256 devices in a mesh: dom: 32 (over x_lo, z, core), ka: 8 (over y, x_hi).
Axes of the slice: x: 4 (x_hi: 2, x_lo: 2; x = x_hi * 2 + x_lo), y: 4, z: 8, core: 2. Of those that a mesh axis runs over, the one named last changes fastest.
Arguments:
- grad_out: bfloat16 [64, 196608], P(None, 'dom'), may hold values from -6 to 6
- frac_pos: float32 [3, 196608], P(None, 'dom'), may hold values from 0 to 1, as said below
- k_index: int32 [3, 4096], P(None, 'ka'), may hold values from -10 to 10
- ewald_filter: float32 [64, 4096], P(None, 'ka'), may hold values from 2.1143198e-05 to 0.00021143198
- struct_fac: float32 [2, 64, 4096], P(None, None, 'ka'), may hold values from -1792 to 1792
- out_weight: bfloat16 [64, 64], replicated, may hold values from -0.75 to 0.75
- pair_mix: bfloat16 [64, 64], replicated, may hold values from -0.75 to 0.75
- pair_weight: float32 [48, 196608], P(None, 'dom'), may hold values from -4 to 4
- nbr_index: int32 [48, 196608], P(None, 'dom'), may hold values from 0 to 7679, as said below
- nbr_count: int32 [196608], P('dom'), may hold values from 12 to 48, as said below
- halo_send: int32 [2, 24576], P(None, 'dom'), may hold values from 0 to 6143, as said below
Outputs:
- d_feat: bfloat16 [64, 196608], P(None, ('dom', 'ka'))
- d_filter: float32 [64, 4096], P(None, 'ka')
The draws below stay inside these ranges and needn't reach their ends.
Inputs may be any that keep to these rules, and one draw needn't show every extreme that they name: `frac_pos`: atoms of a later domain have a larger first coordinate; all coordinates lie in the unit box. The first nbr_count[a] slots of an atom are live. `nbr_index`: a value v below 6144 names the atom at position v of the same domain; 6144 + j names ghost j from the previous domain on the cycle, 6912 + j ghost j from the next domain. `halo_send`: for each domain, 768 positions of its atoms: row 0 those sent to the next domain, row 1 those sent to the previous one.
All inputs are finite; a program needn't handle non-finite values.
Results may differ from the reference program's by a relative error of at most 0.0059.
Values may be sent and summed in bfloat16 or wider, within the bound.
No kernel may reach another device: no remote copies, remote signals or barrier semaphores. Data moves between devices by JAX's collectives and lax.ppermute only.
A program may use at most 128 MiB of HBM per device.

```python
import math
import jax
import jax.numpy as jnp
from jax import lax

CHANNELS = 64
KVEC = 4096
NB = 48
ATOM_DEV = 6144
ATOMS = 196608
HALO = 768
N_DOM = 32


def draw_frac_pos(key, part):
    key = jax.random.fold_in(key, 11)
    key_first, key_rest = jax.random.split(key)
    domain_of = (jnp.arange(ATOMS) // ATOM_DEV).astype(jnp.float32)
    offset = jax.random.uniform(key_first, (ATOMS,), jnp.float32, 0.0, 0.999)
    first_coord = (domain_of + offset) / N_DOM
    others = jax.random.uniform(key_rest, (2, ATOMS), jnp.float32)
    return jnp.concatenate([first_coord[None, :], others], axis=0)


def draw_nbr_count(key, part):
    key = jax.random.fold_in(key, 12)
    counts_drawn = jax.random.randint(key, (ATOMS,), NB // 4, NB + 1)
    full_rows = jnp.arange(ATOMS) % 97 == 0
    return jnp.where(full_rows, NB, counts_drawn).astype(jnp.int32)


def draw_nbr_index(key, part):
    key = jax.random.fold_in(key, 13)
    key_kind, key_local, key_ghost = jax.random.split(key, 3)
    kind_drawn = jax.random.randint(key_kind, (NB, ATOMS), 0, 8)
    local_pick = jax.random.randint(key_local, (NB, ATOMS), 0, ATOM_DEV)
    ghost_pick = jax.random.randint(key_ghost, (NB, ATOMS), 0, HALO)
    chosen = jnp.where(kind_drawn == 6, ATOM_DEV + ghost_pick, jnp.where(kind_drawn == 7, ATOM_DEV + HALO + ghost_pick, local_pick))
    chosen = chosen.at[0, 0].set(ATOM_DEV + 2 * HALO - 1).at[1, 0].set(0)
    return chosen.astype(jnp.int32)


def draw_halo_send(key, part):
    key = jax.random.fold_in(key, 14)
    picks = jax.random.randint(key, (2, HALO * N_DOM), 0, ATOM_DEV)
    picks = picks.at[:, 0].set(ATOM_DEV - 1).at[:, 1].set(0)
    return picks.astype(jnp.int32)


def place_ends(result, rng, low, largest):
    longest = result.shape.index(max(result.shape))
    spots = []
    for shift in (0, 1):
        where = [jax.random.randint(jax.random.fold_in(rng, axis), (), 0, length) for axis, length in enumerate(result.shape)]
        where[longest] = (where[longest] + shift) % result.shape[longest]
        spots.append(tuple(where))
    return result.at[spots[0]].set(low).at[spots[1]].set(largest)


def level_of(stream_key, extent, shards, least, largest):
    gain, own = 1.0, jax.random.fold_in(stream_key, 6)
    for dim, blocks in shards:
        steps = jnp.exp(jax.random.uniform(jax.random.fold_in(own, dim), (blocks,), jnp.float32, least / len(shards), largest / len(shards)))
        gain = gain * jnp.repeat(steps, extent[dim] // blocks).reshape([-1 if axis == dim else 1 for axis in range(len(extent))])
    return gain


def bell_draw(own_key, dims, width, bound, pieces=(), kind=jnp.bfloat16):
    factor_of = level_of(own_key, dims, pieces, -0.22, 0.18) if pieces else 1.0
    result = jax.random.normal(own_key, dims, jnp.float32) * width * factor_of
    return jnp.minimum(jnp.maximum(result, -bound), bound).astype(kind)


def setup_inputs(seed: int = 0) -> dict:
    keys = jax.random.split(jax.random.key(seed), 12)
    grad_out = bell_draw(keys[0], (CHANNELS, ATOMS), 1.0, 6.0, ((1, 32),))
    frac_pos = draw_frac_pos(jax.random.fold_in(keys[11], 71), 0)
    k_index = place_ends(jax.random.randint(keys[2], (3, KVEC), -10, 11), jax.random.fold_in(keys[2], 1), -10, 10).astype(jnp.int32)
    ewald_filter = jnp.clip(jnp.exp(math.log(0.00021143198) - 2.3025851 * jax.random.uniform(keys[3], (CHANNELS, KVEC), jnp.float32) ** level_of(keys[3], (CHANNELS, KVEC), ((1, 8),), -0.2, 0.2)), 2.1143197955098003e-05, 0.00021143198)
    struct_fac = bell_draw(keys[4], (2, CHANNELS, KVEC), (0.7 * ATOMS ** 0.5), 1792.0, ((2, 8),), jnp.float32)
    out_weight = bell_draw(keys[5], (CHANNELS, CHANNELS), CHANNELS ** -0.5, 0.75)
    pair_mix = bell_draw(keys[6], (CHANNELS, CHANNELS), CHANNELS ** -0.5, 0.75)
    pair_weight = bell_draw(keys[7], (NB, ATOMS), 0.25, 4.0, ((1, 32),), jnp.float32)
    nbr_index = draw_nbr_index(jax.random.fold_in(keys[11], 71), 0)
    nbr_count = draw_nbr_count(jax.random.fold_in(keys[11], 71), 0)
    halo_send = draw_halo_send(jax.random.fold_in(keys[11], 71), 0)
    return {"grad_out": grad_out, "frac_pos": frac_pos, "k_index": k_index, "ewald_filter": ewald_filter, "struct_fac": struct_fac, "out_weight": out_weight, "pair_mix": pair_mix, "pair_weight": pair_weight, "nbr_index": nbr_index, "nbr_count": nbr_count, "halo_send": halo_send}


FULL_TURN = 2.0 * math.pi


def phase_pair(frac_block, k_float):
    angles = FULL_TURN * (frac_block[0][:, None] * k_float[0][None, :] + frac_block[1][:, None] * k_float[1][None, :] + frac_block[2][:, None] * k_float[2][None, :])
    return jnp.cos(angles).astype(jnp.bfloat16), jnp.sin(angles).astype(jnp.bfloat16)


def reference(grad_out, frac_pos, k_index, ewald_filter, struct_fac, out_weight, pair_mix, pair_weight, nbr_index, nbr_count, halo_send):
    lr_cot = jnp.dot(out_weight, grad_out, preferred_element_type=jnp.float32).astype(jnp.bfloat16)
    sr_cot = jnp.dot(pair_mix, grad_out, preferred_element_type=jnp.float32).astype(jnp.bfloat16)
    k_float = k_index.astype(jnp.float32)
    block_size = math.gcd(ATOMS, 2048)
    block_count = ATOMS // block_size
    frac_blocks = frac_pos.reshape(3, block_count, block_size).transpose(1, 0, 2)
    cot_blocks = lr_cot.reshape(CHANNELS, block_count, block_size).transpose(1, 0, 2)
    high = lax.Precision.HIGHEST

    def add_block(summed, block_items):
        frac_block, cot_block = block_items
        cos_table, sin_table = phase_pair(frac_block, k_float)
        cot_wide = cot_block.astype(jnp.float32)
        new_cos = summed[0] + jnp.dot(cot_wide, cos_table.astype(jnp.float32), precision=high)
        new_sin = summed[1] + jnp.dot(cot_wide, sin_table.astype(jnp.float32), precision=high)
        return (new_cos, new_sin), None

    zero_k = jnp.zeros((CHANNELS, KVEC), jnp.float32)
    (q_cos, q_sin), _ = lax.scan(add_block, (zero_k, zero_k), (frac_blocks, cot_blocks))
    d_filter = (struct_fac[0] * q_cos + struct_fac[1] * q_sin) / ATOMS
    p_cos = (ewald_filter * q_cos).astype(jnp.bfloat16).astype(jnp.float32)
    p_sin = (ewald_filter * q_sin).astype(jnp.bfloat16).astype(jnp.float32)

    def long_block(frac_block):
        cos_table, sin_table = phase_pair(frac_block, k_float)
        first_part = jnp.dot(p_cos, cos_table.astype(jnp.float32).T, precision=high)
        return first_part + jnp.dot(p_sin, sin_table.astype(jnp.float32).T, precision=high)

    long_blocks = lax.map(long_block, frac_blocks)
    long_term = long_blocks.transpose(1, 0, 2).reshape(CHANNELS, ATOMS)

    atom_ids = jnp.arange(ATOMS, dtype=jnp.int32)
    domain_of = (atom_ids // ATOM_DEV).astype(jnp.int32)
    left_domain = ((domain_of + N_DOM - 1) % N_DOM).astype(jnp.int32)
    right_domain = ((domain_of + 1) % N_DOM).astype(jnp.int32)
    local_ids = nbr_index
    ghost_low = jnp.clip(local_ids - ATOM_DEV, 0, HALO - 1).astype(jnp.int32)
    ghost_high = jnp.clip(local_ids - ATOM_DEV - HALO, 0, HALO - 1).astype(jnp.int32)
    from_left = left_domain[None, :] * ATOM_DEV + halo_send[0][left_domain[None, :] * HALO + ghost_low]
    from_right = right_domain[None, :] * ATOM_DEV + halo_send[1][right_domain[None, :] * HALO + ghost_high]
    own_ids = domain_of[None, :] * ATOM_DEV + jnp.clip(local_ids, 0, ATOM_DEV - 1)
    global_ids = jnp.where(local_ids < ATOM_DEV, own_ids, jnp.where(local_ids < ATOM_DEV + HALO, from_left, from_right)).astype(jnp.int32)
    slot_ids = lax.broadcasted_iota(jnp.int32, (NB, ATOMS), 0)
    weighted = jnp.where(slot_ids < nbr_count[None, :], pair_weight, jnp.zeros_like(pair_weight))

    def add_slot(summed, slot_items):
        slot_weight, slot_atoms = slot_items
        picked = jnp.take(sr_cot, slot_atoms, axis=1).astype(jnp.float32)
        return summed + slot_weight[None, :] * picked, None

    short_term, _ = lax.scan(add_slot, jnp.zeros((CHANNELS, ATOMS), jnp.float32), (weighted, global_ids))
    d_feat = (grad_out.astype(jnp.float32) + long_term + short_term).astype(jnp.bfloat16)
    return d_feat, d_filter
```

```python
import functools
import math

import jax
import jax.numpy as jnp
import numpy as np
from jax import lax
from jax.experimental import pallas as pl
from jax.experimental.pallas import tpu as pltpu
from jax.sharding import PartitionSpec as P

BF16 = jnp.bfloat16
F32 = jnp.float32
LANES = 128


def even_fit(function, terms):
    u = np.cos(np.pi * (np.arange(200) + 0.5) / 200) * 0.125 + 0.125
    fitted = np.polynomial.chebyshev.Chebyshev.fit(u, function(np.sqrt(u)), terms - 1, domain=[0, 0.25])
    return [float(c) for c in fitted.convert(kind=np.polynomial.Polynomial).coef]


SIN_HALF = even_fit(lambda r: math.sqrt(2) * np.sin(np.pi * r) / r, 4)
COS_HALF = even_fit(lambda r: math.sqrt(2) * np.cos(np.pi * r), 4)


def swapped(block, axis, bit):
    return lax.ppermute(block, axis, [(i, i ^ bit) for i in range(lax.axis_size(axis))])


def shifted(block, axis, distance):
    devices = range(lax.axis_size(axis))
    route = [((i - distance) % len(devices), i) for i in devices]
    return lax.ppermute(block, axis, route)


def front_kernel(rows, mix_ref, grad_ref, frac_ref, k_ref, q_ref, table_ref, pieces_ref, turns_ref):
    @pl.when(pl.program_id(0) == 0)
    def _():
        q_ref[...] = jnp.zeros_like(q_ref)
        pieces_ref[...] = jnp.zeros_like(pieces_ref)

    frac = frac_ref[...]
    high = frac.astype(BF16).astype(F32)
    rest = frac - high
    middle = rest.astype(BF16).astype(F32)
    pieces_ref[0:3, :] = high
    pieces_ref[3:6, :] = middle
    pieces_ref[6:9, :] = rest - middle
    turns_ref[...] = jnp.dot(k_ref[...], pieces_ref[...].astype(BF16), preferred_element_type=F32)
    cot = jnp.dot(mix_ref[...], grad_ref[...], preferred_element_type=F32).astype(BF16)
    k_count = k_ref.shape[0]

    def fill(i, carry):
        first = pl.multiple_of(i * rows, rows)
        turns = turns_ref[pl.ds(first, rows), :]
        r = turns - jnp.round(turns)
        u = r * r
        s = r * (SIN_HALF[0] + u * (SIN_HALF[1] + u * (SIN_HALF[2] + u * SIN_HALF[3])))
        c = COS_HALF[0] + u * (COS_HALF[1] + u * (COS_HALF[2] + u * COS_HALF[3]))
        table_ref[pl.ds(first, rows), :] = (1.0 - s * s).astype(BF16)
        table_ref[pl.ds(first + k_count, rows), :] = (s * c).astype(BF16)
        return carry

    lax.fori_loop(0, k_count // rows, fill, 0, unroll=2)
    q_ref[...] += lax.dot_general(
        cot, table_ref[...], (((1,), (1,)), ((), ())), preferred_element_type=F32
    )


def front(mix, grad, frac, k_triple, rows=16, block=1024):
    channels, atoms = grad.shape
    k_count = k_triple.shape[0]
    return pl.pallas_call(
        functools.partial(front_kernel, rows),
        grid=(atoms // block,),
        in_specs=[
            pl.BlockSpec((channels, channels), lambda i: (0, 0)),
            pl.BlockSpec((channels, block), lambda i: (0, i)),
            pl.BlockSpec((3, block), lambda i: (0, i)),
            pl.BlockSpec((k_count, 16), lambda i: (0, 0)),
        ],
        out_specs=[
            pl.BlockSpec((channels, 2 * k_count), lambda i: (0, 0)),
            pl.BlockSpec((2 * k_count, block), lambda i: (0, i)),
        ],
        out_shape=[
            jax.ShapeDtypeStruct((channels, 2 * k_count), F32),
            jax.ShapeDtypeStruct((2 * k_count, atoms), BF16),
        ],
        scratch_shapes=[pltpu.VMEM((16, block), F32), pltpu.VMEM((k_count, block), F32)],
        compiler_params=pltpu.CompilerParams(vmem_limit_bytes=24 << 20),
        cost_estimate=pl.CostEstimate(flops=20_000_000_000, bytes_accessed=14_000_000, transcendentals=0),
        name="structure_sums",
    )(mix, grad, frac, k_triple)


def long_kernel(p_ref, table_ref, out_ref):
    out_ref[0] = jnp.dot(p_ref[...], table_ref[...], preferred_element_type=F32).astype(BF16)


def long_parts(p, table, parts):
    channels, depth = p.shape
    atoms = table.shape[1]
    own = atoms // parts
    return pl.pallas_call(
        long_kernel,
        grid=(parts,),
        in_specs=[
            pl.BlockSpec((channels, depth), lambda i: (0, 0)),
            pl.BlockSpec((depth, own), lambda i: (0, i)),
        ],
        out_specs=pl.BlockSpec((1, channels, own), lambda i: (i, 0, 0)),
        out_shape=jax.ShapeDtypeStruct((parts, channels, own), BF16),
        compiler_params=pltpu.CompilerParams(vmem_limit_bytes=24 << 20),
        cost_estimate=pl.CostEstimate(flops=800_000_000, bytes_accessed=14_000_000, transcendentals=0),
        name="long_parts",
    )(p, table)


def short_kernel(atoms, slots, index_ref, weight_ref, rows_ref, out_ref):
    sublane = lax.broadcasted_iota(jnp.int32, (8, LANES), 0)

    def group(g, carry):
        first = pl.multiple_of(g * 8, 8)
        weights = weight_ref[pl.ds(first, 8), :]
        total = jnp.zeros((8, LANES), F32)
        for s in range(slots):
            picked = jnp.broadcast_to(rows_ref[index_ref[s * atoms + first]], (8, LANES))
            for a in range(1, 8):
                row = jnp.broadcast_to(rows_ref[index_ref[s * atoms + first + a]], (8, LANES))
                picked = jnp.where(sublane == a, row, picked)
            total = total + picked * weights[:, s : s + 1]
        out_ref[pl.ds(first, 8), :] = total
        return carry

    lax.fori_loop(0, atoms // 8, group, 0)


def short_sums(index, weight, rows):
    slots, atoms = index.shape
    return pl.pallas_call(
        functools.partial(short_kernel, atoms, slots),
        in_specs=[
            pl.BlockSpec(memory_space=pltpu.SMEM),
            pl.BlockSpec(memory_space=pltpu.VMEM),
            pl.BlockSpec(memory_space=pltpu.VMEM),
        ],
        out_specs=pl.BlockSpec(memory_space=pltpu.VMEM),
        out_shape=jax.ShapeDtypeStruct((atoms, LANES), F32),
        compiler_params=pltpu.CompilerParams(vmem_limit_bytes=24 << 20),
        cost_estimate=pl.CostEstimate(
            flops=100_000 * slots * atoms, bytes_accessed=4_000_000, transcendentals=0
        ),
        name="short_sums",
    )(index.reshape(-1), weight.T, rows)


def local(
    grad_out,
    frac_pos,
    k_index,
    ewald_filter,
    struct_fac,
    out_weight,
    pair_mix,
    pair_weight,
    nbr_index,
    nbr_count,
    halo_send,
):
    channels, local_atoms = grad_out.shape
    ka_size, dom_size = lax.axis_size("ka"), lax.axis_size("dom")
    own_rows = local_atoms // ka_size
    own_start = lax.axis_index("ka") * own_rows
    k_count = k_index.shape[1]

    mix_wide = jnp.zeros((LANES, channels), BF16).at[:channels].set(pair_mix)
    sr_rows = lax.dot_general(
        grad_out, mix_wide, (((0,), (1,)), ((), ())), preferred_element_type=F32
    ).astype(BF16)
    sr_cot = jnp.dot(pair_mix, grad_out, preferred_element_type=F32).astype(BF16)
    from_left = shifted(jnp.take(sr_cot, halo_send[0], axis=1), "dom", 1)
    from_right = shifted(jnp.take(sr_cot, halo_send[1], axis=1), "dom", -1)
    ghosts = jnp.concatenate([from_left, from_right], axis=1).T
    ghosts = jnp.pad(ghosts, ((0, 0), (0, LANES - channels)))
    extended = jnp.concatenate([sr_rows.astype(F32), ghosts.astype(F32)], axis=0)[:, None, :]

    own_index = lax.dynamic_slice_in_dim(nbr_index, own_start, own_rows, 1)
    own_weight = lax.dynamic_slice_in_dim(pair_weight, own_start, own_rows, 1)
    own_count = lax.dynamic_slice_in_dim(nbr_count, own_start, own_rows, 0)
    slot_ids = lax.broadcasted_iota(jnp.int32, own_index.shape, 0)
    masked = jnp.where(slot_ids < own_count[None, :], own_weight, jnp.zeros_like(own_weight))
    piece_atoms = 128
    short = []

    def beside(value, bit):
        at = len(short) * piece_atoms
        index = own_index[:, at : at + piece_atoms]
        value, index = lax.optimization_barrier((value, index))
        received = swapped(value, "dom", bit)
        piece = short_sums(index, masked[:, at : at + piece_atoms], extended)
        received, piece = lax.optimization_barrier((received, piece))
        short.append(piece)
        return received.astype(F32)

    k_rows = k_index.astype(BF16).T
    k_triple = jnp.concatenate([k_rows, k_rows, k_rows, jnp.zeros((k_count, 7), BF16)], axis=1)
    q, table = front(out_weight, grad_out, frac_pos, k_triple)

    half = channels // 2
    core = lax.axis_index("dom") % 2
    mine = lax.dynamic_slice_in_dim(q, core * half, half, 0)
    other = lax.dynamic_slice_in_dim(q, (1 - core) * half, half, 0)
    total = mine + beside(other.astype(BF16), 1)
    bit = 2
    while bit < dom_size:
        rounded = total.astype(BF16)
        total = rounded.astype(F32) + beside(rounded, bit)
        bit *= 2
    partner = beside(total, 1)
    q = jnp.where(
        core == 0,
        jnp.concatenate([total, partner], axis=0),
        jnp.concatenate([partner, total], axis=0),
    )
    q_cos, q_sin = q[:, :k_count], q[:, k_count:]
    atom_total = local_atoms * dom_size
    d_filter = (struct_fac[0] * q_cos + struct_fac[1] * q_sin) / atom_total
    p = jnp.concatenate([ewald_filter * q_cos, ewald_filter * q_sin], axis=1).astype(BF16)

    parts = lax.all_to_all(long_parts(p, table, ka_size), "ka", 0, 0, tiled=True)
    long_own = jnp.sum(parts.astype(F32), axis=0)
    short_own = jnp.concatenate(short, axis=0)[:, :channels].T
    own_grad = lax.dynamic_slice_in_dim(grad_out, own_start, own_rows, 1).astype(F32)
    d_feat = (own_grad + long_own + short_own).astype(BF16)
    return (d_feat, d_filter)


def solution(mesh):
    return jax.shard_map(
        local,
        mesh=mesh,
        in_specs=(
            P(None, "dom"),
            P(None, "dom"),
            P(None, "ka"),
            P(None, "ka"),
            P(None, None, "ka"),
            P(),
            P(),
            P(None, "dom"),
            P(None, "dom"),
            P("dom"),
            P(None, "dom"),
        ),
        out_specs=(P(None, ("dom", "ka")), P(None, "ka")),
        check_vma=False,
    )
```

```python
import functools
import math

import jax
import jax.numpy as jnp
import numpy as np
from jax import lax
from jax.experimental import pallas as pl
from jax.experimental.pallas import tpu as pltpu
from jax.sharding import PartitionSpec as P

BF16 = jnp.bfloat16
F32 = jnp.float32
LANES = 128


def even_fit(function, terms):
    u = np.cos(np.pi * (np.arange(200) + 0.5) / 200) * 0.125 + 0.125
    fitted = np.polynomial.chebyshev.Chebyshev.fit(u, function(np.sqrt(u)), terms - 1, domain=[0, 0.25])
    return [float(c) for c in fitted.convert(kind=np.polynomial.Polynomial).coef]


SIN_HALF = even_fit(lambda r: math.sqrt(2) * np.sin(np.pi * r) / r, 4)
COS_HALF = even_fit(lambda r: math.sqrt(2) * np.cos(np.pi * r), 4)


def swapped(block, axis, bit):
    return lax.ppermute(block, axis, [(i, i ^ bit) for i in range(lax.axis_size(axis))])


def shifted(block, axis, distance):
    devices = range(lax.axis_size(axis))
    route = [((i - distance) % len(devices), i) for i in devices]
    return lax.ppermute(block, axis, route)


def front_kernel(
    rows, mix_ref, grad_ref, frac_ref, k_ref, q_ref, whole_ref, pieces_ref, turns_ref, held_ref, sems
):
    step, last = pl.program_id(0), pl.num_programs(0) - 1
    slot = lax.rem(step, 2)
    table_ref = held_ref.at[slot]
    block = grad_ref.shape[1]

    def keep(at, slot):
        columns = pl.ds(pl.multiple_of(at * block, block), block)
        return pltpu.make_async_copy(held_ref.at[slot], whole_ref.at[:, columns], sems.at[slot])

    @pl.when(step == 0)
    def _():
        q_ref[...] = jnp.zeros_like(q_ref)
        pieces_ref[...] = jnp.zeros_like(pieces_ref)

    @pl.when(step >= 2)
    def _():
        keep(step - 2, slot).wait()

    frac = frac_ref[...]
    high = frac.astype(BF16).astype(F32)
    rest = frac - high
    middle = rest.astype(BF16).astype(F32)
    pieces_ref[0:3, :] = high
    pieces_ref[3:6, :] = middle
    pieces_ref[6:9, :] = rest - middle
    turns_ref[...] = jnp.dot(k_ref[...], pieces_ref[...].astype(BF16), preferred_element_type=F32)
    cot = jnp.dot(mix_ref[...], grad_ref[...], preferred_element_type=F32).astype(BF16)
    k_count = k_ref.shape[0]

    def fill(i, carry):
        first = pl.multiple_of(i * rows, rows)
        turns = turns_ref[pl.ds(first, rows), :]
        r = turns - jnp.round(turns)
        u = r * r
        s = r * (SIN_HALF[0] + u * (SIN_HALF[1] + u * (SIN_HALF[2] + u * SIN_HALF[3])))
        c = COS_HALF[0] + u * (COS_HALF[1] + u * (COS_HALF[2] + u * COS_HALF[3]))
        table_ref[pl.ds(first, rows), :] = (1.0 - s * s).astype(BF16)
        table_ref[pl.ds(first + k_count, rows), :] = (s * c).astype(BF16)
        return carry

    lax.fori_loop(0, k_count // rows, fill, 0, unroll=2)
    q_ref[...] += lax.dot_general(
        cot, table_ref[...], (((1,), (1,)), ((), ())), preferred_element_type=F32
    )
    keep(step, slot).start()

    @pl.when(step == last)
    def _():
        keep(step - 1, 1 - slot).wait()
        keep(step, slot).wait()


def front(mix, grad, frac, k_triple, rows=16, block=1024):
    channels, atoms = grad.shape
    k_count = k_triple.shape[0]
    return pl.pallas_call(
        functools.partial(front_kernel, rows),
        grid=(atoms // block,),
        in_specs=[
            pl.BlockSpec((channels, channels), lambda i: (0, 0)),
            pl.BlockSpec((channels, block), lambda i: (0, i)),
            pl.BlockSpec((3, block), lambda i: (0, i)),
            pl.BlockSpec((k_count, 16), lambda i: (0, 0)),
        ],
        out_specs=[
            pl.BlockSpec((channels, 2 * k_count), lambda i: (0, 0)),
            pl.BlockSpec(memory_space=pltpu.HBM),
        ],
        out_shape=[
            jax.ShapeDtypeStruct((channels, 2 * k_count), F32),
            pltpu.HBM((2 * k_count, atoms), BF16),
        ],
        scratch_shapes=[
            pltpu.VMEM((16, block), F32),
            pltpu.VMEM((k_count, block), F32),
            pltpu.VMEM((2, 2 * k_count, block), BF16),
            pltpu.SemaphoreType.DMA((2,)),
        ],
        compiler_params=pltpu.CompilerParams(vmem_limit_bytes=12 << 20),
        cost_estimate=pl.CostEstimate(flops=20_000_000_000, bytes_accessed=14_000_000, transcendentals=0),
        name="structure_sums",
    )(mix, grad, frac, k_triple)


def long_kernel(p_ref, table_ref, out_ref, held_ref, sems):
    parts, _, own = out_ref.shape
    depth = held_ref.shape[0]

    def fetch(at):
        columns = slice(at * own, (at + 1) * own)
        return pltpu.make_async_copy(
            table_ref.at[:, columns], held_ref.at[at % depth], sems.at[at % depth]
        )

    for at in range(depth - 1):
        fetch(at).start()
    for at in range(parts):
        if at + depth - 1 < parts:
            fetch(at + depth - 1).start()
        fetch(at).wait()
        out_ref[at] = jnp.dot(
            p_ref[...], held_ref[at % depth], preferred_element_type=F32
        ).astype(BF16)


def long_parts(p, table, parts):
    channels, depth = p.shape
    own = table.shape[1] // parts
    return pl.pallas_call(
        long_kernel,
        in_specs=[pl.BlockSpec(memory_space=pltpu.VMEM), pl.BlockSpec(memory_space=pltpu.HBM)],
        out_specs=pl.BlockSpec(memory_space=pltpu.VMEM),
        out_shape=jax.ShapeDtypeStruct((parts, channels, own), BF16),
        scratch_shapes=[pltpu.VMEM((4, depth, own), BF16), pltpu.SemaphoreType.DMA((4,))],
        compiler_params=pltpu.CompilerParams(vmem_limit_bytes=12 << 20),
        cost_estimate=pl.CostEstimate(flops=800_000_000, bytes_accessed=14_000_000, transcendentals=0),
        name="long_parts",
    )(p, table)


def prepare_kernel(
    ka_ref, halo_ref, mix_ref, grad_ref, index_ref, weight_ref, count_ref,
    rows_ref, send_ref, slots_ref, masked_ref, picked_ref,
):
    atoms = grad_ref.shape[1]
    block = math.gcd(atoms, 512)
    sends, per_side = send_ref.shape[0], halo_ref.shape[1]

    def mix(i, carry):
        first = pl.multiple_of(i * block, block)
        mixed = lax.dot_general(
            grad_ref[:, pl.ds(first, block)], mix_ref[...], (((0,), (1,)), ((), ())),
            preferred_element_type=F32,
        )
        rows_ref[pl.ds(first, block), :] = mixed.astype(BF16).astype(F32)
        return carry

    lax.fori_loop(0, atoms // block, mix, 0)

    for side in range(2):
        def pick(i, carry, side=side):
            first = pl.multiple_of(i * 32, 32)
            for j in range(32):
                picked_ref[pl.ds(side * per_side + first + j, 1), :] = rows_ref[
                    pl.ds(halo_ref[side, first + j], 1), :
                ]
            return carry

        lax.fori_loop(0, per_side // 32, pick, 0)
    send_ref[...] = picked_ref[...].astype(BF16)

    slot = lax.broadcasted_iota(jnp.int32, weight_ref.shape, 0)
    masked = jnp.where(slot < count_ref[...], weight_ref[...], 0.0)
    for piece in range(slots_ref.shape[0]):
        cut = slice(piece * LANES, (piece + 1) * LANES)
        slots_ref[piece] = index_ref[:, cut]
        masked_ref[cut, :] = masked[:, cut].T


def prepare(ka, mix_wide, grad, index, weight, count, halo):
    channels, atoms = grad.shape
    slots = index.shape[0]
    per_side = halo.shape[1]
    own = atoms // lax.axis_size("ka")
    whole = pl.BlockSpec(memory_space=pltpu.VMEM)
    return pl.pallas_call(
        prepare_kernel,
        grid_spec=pltpu.PrefetchScalarGridSpec(
            num_scalar_prefetch=1,
            grid=(1,),
            in_specs=[
                pl.BlockSpec(memory_space=pltpu.SMEM),
                whole,
                whole,
                pl.BlockSpec((slots, own), lambda i, ka: (0, ka[0])),
                pl.BlockSpec((slots, own), lambda i, ka: (0, ka[0])),
                pl.BlockSpec((1, own), lambda i, ka: (0, ka[0])),
            ],
            out_specs=[whole, whole, whole, whole],
            scratch_shapes=[pltpu.VMEM((2 * per_side, LANES), F32)],
        ),
        out_shape=[
            jax.ShapeDtypeStruct((atoms + 2 * per_side, LANES), F32),
            jax.ShapeDtypeStruct((2 * per_side, LANES), BF16),
            jax.ShapeDtypeStruct((own // LANES, slots, LANES), jnp.int32),
            jax.ShapeDtypeStruct((own, slots), F32),
        ],
        compiler_params=pltpu.CompilerParams(vmem_limit_bytes=12 << 20),
        cost_estimate=pl.CostEstimate(flops=1_000_000_000, bytes_accessed=8_000_000, transcendentals=0),
        name="prepare",
    )(ka, halo, mix_wide, grad, index, weight, count)


def short_kernel(index_ref, weight_ref, rows_ref, out_ref, sums_ref):
    sublane = lax.broadcasted_iota(jnp.int32, (8, LANES), 0)

    def group(g, carry):
        first = pl.multiple_of(g * 8, 8)
        weights = weight_ref[pl.ds(first, 8), :]
        total = jnp.zeros((8, LANES), F32)
        for s in range(index_ref.shape[1]):
            picked = jnp.broadcast_to(rows_ref[index_ref[0, s, first]], (8, LANES))
            for a in range(1, 8):
                row = jnp.broadcast_to(rows_ref[index_ref[0, s, first + a]], (8, LANES))
                picked = jnp.where(sublane == a, row, picked)
            total = total + picked * weights[:, s : s + 1]
        sums_ref[pl.ds(first, 8), :] = total
        return carry

    lax.fori_loop(0, LANES // 8, group, 0)
    out_ref[...] = sums_ref[...].T[: out_ref.shape[0], :]


def short_sums(piece, channels, index, weight, rows):
    slots = index.shape[1]
    return pl.pallas_call(
        short_kernel,
        grid=(1,),
        in_specs=[
            pl.BlockSpec((1, slots, LANES), lambda i: (piece, 0, 0), memory_space=pltpu.SMEM),
            pl.BlockSpec((LANES, slots), lambda i: (piece, 0)),
            pl.BlockSpec(memory_space=pltpu.VMEM),
        ],
        out_specs=pl.BlockSpec(memory_space=pltpu.VMEM),
        out_shape=jax.ShapeDtypeStruct((channels, LANES), F32),
        scratch_shapes=[pltpu.VMEM((LANES, LANES), F32)],
        compiler_params=pltpu.CompilerParams(vmem_limit_bytes=6 << 20),
        cost_estimate=pl.CostEstimate(flops=4_000_000_000, bytes_accessed=4_000_000, transcendentals=0),
        name="short_sums",
    )(index, weight, rows)


def local(
    grad_out,
    frac_pos,
    k_index,
    ewald_filter,
    struct_fac,
    out_weight,
    pair_mix,
    pair_weight,
    nbr_index,
    nbr_count,
    halo_send,
):
    channels, local_atoms = grad_out.shape
    ka_size, dom_size = lax.axis_size("ka"), lax.axis_size("dom")
    own_rows = local_atoms // ka_size
    k_count = k_index.shape[1]

    ka = lax.axis_index("ka").astype(jnp.int32)
    mix_wide = jnp.pad(pair_mix, ((0, LANES - channels), (0, 0)))
    rows, send, slots, masked = prepare(
        ka[None], mix_wide, grad_out, nbr_index, pair_weight, nbr_count[None, :], halo_send
    )
    per_side = halo_send.shape[1]
    from_left = shifted(send[:per_side], "dom", 1)
    from_right = shifted(send[per_side:], "dom", -1)
    short = []

    def short_piece():
        short.append(short_sums(len(short), channels, slots, masked, extended))

    def beside(value, bit, pieces):
        nonlocal slots
        value, slots = lax.optimization_barrier((value, slots))
        received = swapped(value, "dom", bit)
        start = len(short)
        for _ in range(pieces):
            short_piece()
        received, short[start:] = lax.optimization_barrier((received, short[start:]))
        return received.astype(F32)

    k_rows = k_index.astype(BF16).T
    k_triple = jnp.concatenate([k_rows, k_rows, k_rows, jnp.zeros((k_count, 7), BF16)], axis=1)
    frac_late, send_late = lax.optimization_barrier((frac_pos, send))
    q, table = front(out_weight, grad_out, frac_late, k_triple)
    q, from_left, from_right = lax.optimization_barrier((q, from_left, from_right))
    extended = jnp.concatenate(
        [rows[:local_atoms], from_left.astype(F32), from_right.astype(F32)], axis=0
    )[:, None, :]

    half = channels // 2
    core = lax.axis_index("dom") % 2
    mine = lax.dynamic_slice_in_dim(q, core * half, half, 0)
    other = lax.dynamic_slice_in_dim(q, (1 - core) * half, half, 0)
    total = mine + beside(other.astype(BF16), 1, 0)
    bit = 2
    while bit < dom_size:
        rounded = total.astype(BF16)
        total = rounded.astype(F32) + beside(rounded, bit, 1)
        bit *= 2
    partner = beside(total, 1, 0)
    q = jnp.where(
        core == 0,
        jnp.concatenate([total, partner], axis=0),
        jnp.concatenate([partner, total], axis=0),
    )
    q_cos, q_sin = q[:, :k_count], q[:, k_count:]
    atom_total = local_atoms * dom_size
    d_filter = (struct_fac[0] * q_cos + struct_fac[1] * q_sin) / atom_total
    p = jnp.concatenate([ewald_filter * q_cos, ewald_filter * q_sin], axis=1).astype(BF16)

    parts = long_parts(p, table, ka_size)
    parts, slots = lax.optimization_barrier((parts, slots))
    parts = lax.all_to_all(parts, "ka", 0, 0, tiled=True)
    while len(short) < own_rows // LANES:
        short_piece()
    long_own = jnp.sum(parts.astype(F32), axis=0)
    own_grad = lax.dynamic_slice_in_dim(grad_out, ka * own_rows, own_rows, 1).astype(F32)
    d_feat = (own_grad + long_own + jnp.concatenate(short, axis=1)).astype(BF16)
    return (d_feat, d_filter)


def solution(mesh):
    return jax.shard_map(
        local,
        mesh=mesh,
        in_specs=(
            P(None, "dom"),
            P(None, "dom"),
            P(None, "ka"),
            P(None, "ka"),
            P(None, None, "ka"),
            P(),
            P(),
            P(None, "dom"),
            P(None, "dom"),
            P("dom"),
            P(None, "dom"),
        ),
        out_specs=(P(None, ("dom", "ka")), P(None, "ka")),
        check_vma=False,
    )
```

```python
import functools
import math

import jax
import jax.numpy as jnp
import numpy as np
from jax import lax
from jax.experimental import pallas as pl
from jax.experimental.pallas import tpu as pltpu
from jax.sharding import PartitionSpec as P

BF16 = jnp.bfloat16
F32 = jnp.float32
LANES = 128


def even_fit(function, terms):
    u = np.cos(np.pi * (np.arange(200) + 0.5) / 200) * 0.125 + 0.125
    fitted = np.polynomial.chebyshev.Chebyshev.fit(u, function(np.sqrt(u)), terms - 1, domain=[0, 0.25])
    return [float(c) for c in fitted.convert(kind=np.polynomial.Polynomial).coef]


SIN_HALF = even_fit(lambda r: math.sqrt(2) * np.sin(np.pi * r) / r, 4)
COS_HALF = even_fit(lambda r: math.sqrt(2) * np.cos(np.pi * r), 4)


def swapped(block, axis, bit):
    return lax.ppermute(block, axis, [(i, i ^ bit) for i in range(lax.axis_size(axis))])


def shifted(block, axis, distance):
    devices = range(lax.axis_size(axis))
    route = [((i - distance) % len(devices), i) for i in devices]
    return lax.ppermute(block, axis, route)


def front_kernel(
    rows, mix_ref, grad_ref, frac_ref, k_ref, q_ref, whole_ref, pieces_ref, turns_ref, held_ref, sems
):
    step, last = pl.program_id(0), pl.num_programs(0) - 1
    slot = lax.rem(step, 2)
    table_ref = held_ref.at[slot]
    block = grad_ref.shape[1]

    def keep(at, slot):
        columns = pl.ds(pl.multiple_of(at * block, block), block)
        return pltpu.make_async_copy(held_ref.at[slot], whole_ref.at[:, columns], sems.at[slot])

    @pl.when(step == 0)
    def _():
        q_ref[...] = jnp.zeros_like(q_ref)
        pieces_ref[...] = jnp.zeros_like(pieces_ref)

    @pl.when(step >= 2)
    def _():
        keep(step - 2, slot).wait()

    frac = frac_ref[...]
    high = frac.astype(BF16).astype(F32)
    rest = frac - high
    middle = rest.astype(BF16).astype(F32)
    pieces_ref[0:3, :] = high
    pieces_ref[3:6, :] = middle
    pieces_ref[6:9, :] = rest - middle
    turns_ref[...] = jnp.dot(k_ref[...], pieces_ref[...].astype(BF16), preferred_element_type=F32)
    cot = jnp.dot(mix_ref[...], grad_ref[...], preferred_element_type=F32).astype(BF16)
    k_count = k_ref.shape[0]

    def fill(i, carry):
        first = pl.multiple_of(i * rows, rows)
        turns = turns_ref[pl.ds(first, rows), :]
        r = turns - jnp.round(turns)
        u = r * r
        s = r * (SIN_HALF[0] + u * (SIN_HALF[1] + u * (SIN_HALF[2] + u * SIN_HALF[3])))
        c = COS_HALF[0] + u * (COS_HALF[1] + u * (COS_HALF[2] + u * COS_HALF[3]))
        table_ref[pl.ds(first, rows), :] = (1.0 - s * s).astype(BF16)
        table_ref[pl.ds(first + k_count, rows), :] = (s * c).astype(BF16)
        return carry

    lax.fori_loop(0, k_count // rows, fill, 0, unroll=2)
    q_ref[...] += lax.dot_general(
        cot, table_ref[...], (((1,), (1,)), ((), ())), preferred_element_type=F32
    )
    keep(step, slot).start()

    @pl.when(step == last)
    def _():
        keep(step - 1, 1 - slot).wait()
        keep(step, slot).wait()


def front(mix, grad, frac, k_triple, rows=16, block=1024):
    channels, atoms = grad.shape
    k_count = k_triple.shape[0]
    return pl.pallas_call(
        functools.partial(front_kernel, rows),
        grid=(atoms // block,),
        in_specs=[
            pl.BlockSpec((channels, channels), lambda i: (0, 0)),
            pl.BlockSpec((channels, block), lambda i: (0, i)),
            pl.BlockSpec((3, block), lambda i: (0, i)),
            pl.BlockSpec((k_count, 16), lambda i: (0, 0)),
        ],
        out_specs=[
            pl.BlockSpec((channels, 2 * k_count), lambda i: (0, 0)),
            pl.BlockSpec(memory_space=pltpu.HBM),
        ],
        out_shape=[
            jax.ShapeDtypeStruct((channels, 2 * k_count), F32),
            pltpu.HBM((2 * k_count, atoms), BF16),
        ],
        scratch_shapes=[
            pltpu.VMEM((16, block), F32),
            pltpu.VMEM((k_count, block), F32),
            pltpu.VMEM((2, 2 * k_count, block), BF16),
            pltpu.SemaphoreType.DMA((2,)),
        ],
        compiler_params=pltpu.CompilerParams(vmem_limit_bytes=12 << 20),
        cost_estimate=pl.CostEstimate(flops=20_000_000_000, bytes_accessed=14_000_000, transcendentals=0),
        name="structure_sums",
    )(mix, grad, frac, k_triple)


def long_kernel(p_ref, table_ref, out_ref, held_ref, sems):
    parts, _, own = out_ref.shape
    depth = held_ref.shape[0]

    def fetch(at):
        columns = slice(at * own, (at + 1) * own)
        return pltpu.make_async_copy(
            table_ref.at[:, columns], held_ref.at[at % depth], sems.at[at % depth]
        )

    for at in range(depth - 1):
        fetch(at).start()
    for at in range(parts):
        if at + depth - 1 < parts:
            fetch(at + depth - 1).start()
        fetch(at).wait()
        out_ref[at] = jnp.dot(
            p_ref[...], held_ref[at % depth], preferred_element_type=F32
        ).astype(BF16)


def long_parts(p, table, parts):
    channels, depth = p.shape
    own = table.shape[1] // parts
    return pl.pallas_call(
        long_kernel,
        in_specs=[pl.BlockSpec(memory_space=pltpu.VMEM), pl.BlockSpec(memory_space=pltpu.HBM)],
        out_specs=pl.BlockSpec(memory_space=pltpu.VMEM),
        out_shape=jax.ShapeDtypeStruct((parts, channels, own), BF16),
        scratch_shapes=[pltpu.VMEM((4, depth, own), BF16), pltpu.SemaphoreType.DMA((4,))],
        compiler_params=pltpu.CompilerParams(vmem_limit_bytes=12 << 20),
        cost_estimate=pl.CostEstimate(flops=800_000_000, bytes_accessed=14_000_000, transcendentals=0),
        name="long_parts",
    )(p, table)


def prepare_kernel(
    ka_ref, halo_ref, mix_ref, grad_ref, index_ref, weight_ref, count_ref,
    rows_ref, send_ref, masked_ref, *refs,
):
    *slots_refs, picked_ref = refs
    atoms = grad_ref.shape[1]
    block = math.gcd(atoms, 512)
    sends, per_side = send_ref.shape[0], halo_ref.shape[1]

    def mix(i, carry):
        first = pl.multiple_of(i * block, block)
        mixed = lax.dot_general(
            grad_ref[:, pl.ds(first, block)], mix_ref[...], (((0,), (1,)), ((), ())),
            preferred_element_type=F32,
        )
        rows_ref[pl.ds(first, block), :] = mixed.astype(BF16).astype(F32)
        return carry

    lax.fori_loop(0, atoms // block, mix, 0)

    for side in range(2):
        def pick(i, carry, side=side):
            first = pl.multiple_of(i * 32, 32)
            for j in range(32):
                picked_ref[pl.ds(side * per_side + first + j, 1), :] = rows_ref[
                    pl.ds(halo_ref[side, first + j], 1), :
                ]
            return carry

        lax.fori_loop(0, per_side // 32, pick, 0)
    send_ref[...] = picked_ref[...].astype(BF16)

    slot = lax.broadcasted_iota(jnp.int32, weight_ref.shape, 0)
    masked = jnp.where(slot < count_ref[...], weight_ref[...], 0.0)
    for piece, slots_ref in enumerate(slots_refs):
        cut = slice(piece * LANES, (piece + 1) * LANES)
        slots_ref[...] = index_ref[:, cut]
        masked_ref[cut, :] = masked[:, cut].T


def prepare(ka, mix_wide, grad, index, weight, count, halo):
    channels, atoms = grad.shape
    slots = index.shape[0]
    per_side = halo.shape[1]
    own = atoms // lax.axis_size("ka")
    whole = pl.BlockSpec(memory_space=pltpu.VMEM)
    return pl.pallas_call(
        prepare_kernel,
        grid_spec=pltpu.PrefetchScalarGridSpec(
            num_scalar_prefetch=1,
            grid=(1,),
            in_specs=[
                pl.BlockSpec(memory_space=pltpu.SMEM),
                whole,
                whole,
                pl.BlockSpec((slots, own), lambda i, ka: (0, ka[0])),
                pl.BlockSpec((slots, own), lambda i, ka: (0, ka[0])),
                pl.BlockSpec((1, own), lambda i, ka: (0, ka[0])),
            ],
            out_specs=[whole] * (3 + own // LANES),
            scratch_shapes=[pltpu.VMEM((2 * per_side, LANES), F32)],
        ),
        out_shape=[
            jax.ShapeDtypeStruct((atoms + 2 * per_side, LANES), F32),
            jax.ShapeDtypeStruct((2 * per_side, LANES), BF16),
            jax.ShapeDtypeStruct((own, slots), F32),
        ]
        + [jax.ShapeDtypeStruct((slots, LANES), jnp.int32)] * (own // LANES),
        compiler_params=pltpu.CompilerParams(vmem_limit_bytes=12 << 20),
        cost_estimate=pl.CostEstimate(flops=1_000_000_000, bytes_accessed=8_000_000, transcendentals=0),
        name="prepare",
    )(ka, halo, mix_wide, grad, index, weight, count)


def short_kernel(index_ref, weight_ref, rows_ref, out_ref, sums_ref):
    sublane = lax.broadcasted_iota(jnp.int32, (8, LANES), 0)

    def group(g, carry):
        first = pl.multiple_of(g * 8, 8)
        weights = weight_ref[pl.ds(first, 8), :]
        total = jnp.zeros((8, LANES), F32)
        for s in range(weight_ref.shape[1]):
            picked = jnp.broadcast_to(rows_ref[index_ref[s * LANES + first]], (8, LANES))
            for a in range(1, 8):
                row = jnp.broadcast_to(rows_ref[index_ref[s * LANES + first + a]], (8, LANES))
                picked = jnp.where(sublane == a, row, picked)
            total = total + picked * weights[:, s : s + 1]
        sums_ref[pl.ds(first, 8), :] = total
        return carry

    lax.fori_loop(0, LANES // 8, group, 0)
    out_ref[...] = sums_ref[...].T[: out_ref.shape[0], :]


def short_sums(piece, channels, index, weight, rows):
    slots = weight.shape[1]
    return pl.pallas_call(
        short_kernel,
        grid=(1,),
        in_specs=[
            pl.BlockSpec(memory_space=pltpu.SMEM),
            pl.BlockSpec((LANES, slots), lambda i: (piece, 0)),
            pl.BlockSpec(memory_space=pltpu.VMEM),
        ],
        out_specs=pl.BlockSpec(memory_space=pltpu.VMEM),
        out_shape=jax.ShapeDtypeStruct((channels, LANES), F32),
        scratch_shapes=[pltpu.VMEM((LANES, LANES), F32)],
        compiler_params=pltpu.CompilerParams(vmem_limit_bytes=6 << 20),
        cost_estimate=pl.CostEstimate(flops=4_000_000_000, bytes_accessed=4_000_000, transcendentals=0),
        name="short_sums",
    )(index, weight, rows)


def local(
    grad_out,
    frac_pos,
    k_index,
    ewald_filter,
    struct_fac,
    out_weight,
    pair_mix,
    pair_weight,
    nbr_index,
    nbr_count,
    halo_send,
):
    channels, local_atoms = grad_out.shape
    ka_size, dom_size = lax.axis_size("ka"), lax.axis_size("dom")
    own_rows = local_atoms // ka_size
    k_count = k_index.shape[1]

    ka = lax.axis_index("ka").astype(jnp.int32)
    mix_wide = jnp.pad(pair_mix, ((0, LANES - channels), (0, 0)))
    rows, send, masked, *slots = prepare(
        ka[None],
        mix_wide,
        grad_out,
        pltpu.with_memory_space_constraint(nbr_index, pltpu.HBM),
        pltpu.with_memory_space_constraint(pair_weight, pltpu.HBM),
        nbr_count[None, :],
        halo_send,
    )
    per_side = halo_send.shape[1]
    from_left = shifted(send[:per_side], "dom", 1)
    from_right = shifted(send[per_side:], "dom", -1)
    short = []

    def short_piece():
        piece = len(short)
        short.append(short_sums(piece, channels, slots[piece].reshape(-1), masked, extended))

    def beside(value, bit, pieces):
        nonlocal slots
        value, slots = lax.optimization_barrier((value, slots))
        received = swapped(value, "dom", bit)
        start = len(short)
        for _ in range(pieces):
            short_piece()
        received, short[start:] = lax.optimization_barrier((received, short[start:]))
        return received.astype(F32)

    k_rows = k_index.astype(BF16).T
    k_triple = jnp.concatenate([k_rows, k_rows, k_rows, jnp.zeros((k_count, 7), BF16)], axis=1)
    frac_late, send_late = lax.optimization_barrier((frac_pos, send))
    q, table = front(out_weight, grad_out, frac_late, k_triple)
    q, from_left, from_right = lax.optimization_barrier((q, from_left, from_right))
    ghosts = jnp.concatenate([from_left, from_right], axis=0).astype(F32)
    extended = lax.dynamic_update_slice_in_dim(rows, ghosts, local_atoms, 0)
    extended = lax.optimization_barrier(extended)[:, None, :]

    half = channels // 2
    core = lax.axis_index("dom") % 2
    mine = lax.dynamic_slice_in_dim(q, core * half, half, 0)
    other = lax.dynamic_slice_in_dim(q, (1 - core) * half, half, 0)
    total = mine + beside(other.astype(BF16), 1, 0)
    bit = 2
    while bit < dom_size:
        rounded = total.astype(BF16)
        total = rounded.astype(F32) + beside(rounded, bit, 0 if bit == 8 else 1)
        bit *= 2
    partner = beside(total, 1, 0)
    q = jnp.where(
        core == 0,
        jnp.concatenate([total, partner], axis=0),
        jnp.concatenate([partner, total], axis=0),
    )
    q_cos, q_sin = q[:, :k_count], q[:, k_count:]
    atom_total = local_atoms * dom_size
    d_filter = (struct_fac[0] * q_cos + struct_fac[1] * q_sin) / atom_total
    p = jnp.concatenate([ewald_filter * q_cos, ewald_filter * q_sin], axis=1).astype(BF16)

    table = pltpu.with_memory_space_constraint(table, pltpu.HBM)
    parts = long_parts(p, table, ka_size)
    parts, slots = lax.optimization_barrier((parts, slots))
    parts = lax.all_to_all(parts, "ka", 0, 0, tiled=True)
    while len(short) < own_rows // LANES:
        short_piece()
    long_own = jnp.sum(parts.astype(F32), axis=0)
    own_grad = lax.dynamic_slice_in_dim(grad_out, ka * own_rows, own_rows, 1).astype(F32)
    d_feat = (own_grad + long_own + jnp.concatenate(short, axis=1)).astype(BF16)
    return (d_feat, d_filter)


def solution(mesh):
    return jax.shard_map(
        local,
        mesh=mesh,
        in_specs=(
            P(None, "dom"),
            P(None, "dom"),
            P(None, "ka"),
            P(None, "ka"),
            P(None, None, "ka"),
            P(),
            P(),
            P(None, "dom"),
            P(None, "dom"),
            P("dom"),
            P(None, "dom"),
        ),
        out_specs=(P(None, ("dom", "ka")), P(None, "ka")),
        check_vma=False,
    )
```

```python
import functools
import math

import jax
import jax.numpy as jnp
import numpy as np
from jax import lax
from jax.experimental import pallas as pl
from jax.experimental.pallas import tpu as pltpu
from jax.sharding import PartitionSpec as P

BF16 = jnp.bfloat16
F32 = jnp.float32
LANES = 128


def even_fit(function, terms):
    u = np.cos(np.pi * (np.arange(200) + 0.5) / 200) * 0.125 + 0.125
    fitted = np.polynomial.chebyshev.Chebyshev.fit(u, function(np.sqrt(u)), terms - 1, domain=[0, 0.25])
    return [float(c) for c in fitted.convert(kind=np.polynomial.Polynomial).coef]


SIN_HALF = even_fit(lambda r: math.sqrt(2) * np.sin(np.pi * r) / r, 4)
COS_HALF = even_fit(lambda r: math.sqrt(2) * np.cos(np.pi * r), 4)


def swapped(block, axis, bit):
    return lax.ppermute(block, axis, [(i, i ^ bit) for i in range(lax.axis_size(axis))])


def shifted(block, axis, distance):
    devices = range(lax.axis_size(axis))
    route = [((i - distance) % len(devices), i) for i in devices]
    return lax.ppermute(block, axis, route)


def front_kernel(
    rows, mix_ref, grad_ref, frac_ref, k_ref, q_ref, whole_ref, pieces_ref, turns_ref, held_ref, sems
):
    step, last = pl.program_id(0), pl.num_programs(0) - 1
    slot = lax.rem(step, 2)
    table_ref = held_ref.at[slot]
    block = grad_ref.shape[1]

    def keep(at, slot):
        columns = pl.ds(pl.multiple_of(at * block, block), block)
        return pltpu.make_async_copy(held_ref.at[slot], whole_ref.at[:, columns], sems.at[slot])

    @pl.when(step == 0)
    def _():
        q_ref[...] = jnp.zeros_like(q_ref)
        pieces_ref[...] = jnp.zeros_like(pieces_ref)

    @pl.when(step >= 2)
    def _():
        keep(step - 2, slot).wait()

    frac = frac_ref[...]
    high = frac.astype(BF16).astype(F32)
    rest = frac - high
    middle = rest.astype(BF16).astype(F32)
    pieces_ref[0:3, :] = high
    pieces_ref[3:6, :] = middle
    pieces_ref[6:9, :] = rest - middle
    turns_ref[...] = jnp.dot(k_ref[...], pieces_ref[...].astype(BF16), preferred_element_type=F32)
    cot = jnp.dot(mix_ref[...], grad_ref[...], preferred_element_type=F32).astype(BF16)
    k_count = k_ref.shape[0]

    def fill(i, carry):
        first = pl.multiple_of(i * rows, rows)
        turns = turns_ref[pl.ds(first, rows), :]
        r = turns - jnp.round(turns)
        u = r * r
        s = r * (SIN_HALF[0] + u * (SIN_HALF[1] + u * (SIN_HALF[2] + u * SIN_HALF[3])))
        c = COS_HALF[0] + u * (COS_HALF[1] + u * (COS_HALF[2] + u * COS_HALF[3]))
        table_ref[pl.ds(first, rows), :] = (1.0 - s * s).astype(BF16)
        table_ref[pl.ds(first + k_count, rows), :] = (s * c).astype(BF16)
        return carry

    lax.fori_loop(0, k_count // rows, fill, 0, unroll=2)
    q_ref[...] += lax.dot_general(
        cot, table_ref[...], (((1,), (1,)), ((), ())), preferred_element_type=F32
    )
    keep(step, slot).start()

    @pl.when(step == last)
    def _():
        keep(step - 1, 1 - slot).wait()
        keep(step, slot).wait()


def front(mix, grad, frac, k_triple, rows=16, block=1024):
    channels, atoms = grad.shape
    k_count = k_triple.shape[0]
    return pl.pallas_call(
        functools.partial(front_kernel, rows),
        grid=(atoms // block,),
        in_specs=[
            pl.BlockSpec((channels, channels), lambda i: (0, 0)),
            pl.BlockSpec((channels, block), lambda i: (0, i)),
            pl.BlockSpec((3, block), lambda i: (0, i)),
            pl.BlockSpec((k_count, 16), lambda i: (0, 0)),
        ],
        out_specs=[
            pl.BlockSpec((channels, 2 * k_count), lambda i: (0, 0)),
            pl.BlockSpec(memory_space=pltpu.HBM),
        ],
        out_shape=[
            jax.ShapeDtypeStruct((channels, 2 * k_count), F32),
            pltpu.HBM((2 * k_count, atoms), BF16),
        ],
        scratch_shapes=[
            pltpu.VMEM((16, block), F32),
            pltpu.VMEM((k_count, block), F32),
            pltpu.VMEM((2, 2 * k_count, block), BF16),
            pltpu.SemaphoreType.DMA((2,)),
        ],
        compiler_params=pltpu.CompilerParams(vmem_limit_bytes=12 << 20),
        cost_estimate=pl.CostEstimate(flops=20_000_000_000, bytes_accessed=14_000_000, transcendentals=0),
        name="structure_sums",
    )(mix, grad, frac, k_triple)


def long_kernel(p_ref, table_ref, out_ref, held_ref, sems):
    parts, _, own = out_ref.shape
    depth = held_ref.shape[0]

    def fetch(at):
        columns = slice(at * own, (at + 1) * own)
        return pltpu.make_async_copy(
            table_ref.at[:, columns], held_ref.at[at % depth], sems.at[at % depth]
        )

    for at in range(depth - 1):
        fetch(at).start()
    for at in range(parts):
        if at + depth - 1 < parts:
            fetch(at + depth - 1).start()
        fetch(at).wait()
        out_ref[at] = jnp.dot(
            p_ref[...], held_ref[at % depth], preferred_element_type=F32
        ).astype(BF16)


def long_parts(p, table, parts):
    channels, depth = p.shape
    own = table.shape[1] // parts
    return pl.pallas_call(
        long_kernel,
        in_specs=[pl.BlockSpec(memory_space=pltpu.VMEM), pl.BlockSpec(memory_space=pltpu.HBM)],
        out_specs=pl.BlockSpec(memory_space=pltpu.VMEM),
        out_shape=jax.ShapeDtypeStruct((parts, channels, own), BF16),
        scratch_shapes=[pltpu.VMEM((4, depth, own), BF16), pltpu.SemaphoreType.DMA((4,))],
        compiler_params=pltpu.CompilerParams(vmem_limit_bytes=12 << 20),
        cost_estimate=pl.CostEstimate(flops=800_000_000, bytes_accessed=14_000_000, transcendentals=0),
        name="long_parts",
    )(p, table)


def prepare_kernel(
    ka_ref, halo_ref, mix_ref, grad_ref, index_ref, weight_ref, count_ref,
    rows_ref, send_ref, masked_ref, *refs,
):
    *slots_refs, picked_ref, held_ref, sem = refs
    atoms = grad_ref.shape[1]
    block = math.gcd(atoms, 512)
    sends, per_side = send_ref.shape[0], halo_ref.shape[1]

    def mix(i, carry):
        first = pl.multiple_of(i * block, block)
        mixed = lax.dot_general(
            grad_ref[:, pl.ds(first, block)], mix_ref[...], (((0,), (1,)), ((), ())),
            preferred_element_type=F32,
        )
        held_ref[pl.ds(first, block), :] = mixed.astype(BF16).astype(F32)
        return carry

    lax.fori_loop(0, atoms // block, mix, 0)
    leave = pltpu.make_async_copy(held_ref, rows_ref.at[pl.ds(0, atoms)], sem)
    leave.start()

    for side in range(2):
        def pick(i, carry, side=side):
            first = pl.multiple_of(i * 32, 32)
            for j in range(32):
                picked_ref[pl.ds(side * per_side + first + j, 1), :] = held_ref[
                    pl.ds(halo_ref[side, first + j], 1), :
                ]
            return carry

        lax.fori_loop(0, per_side // 32, pick, 0)
    send_ref[...] = picked_ref[...].astype(BF16)

    slot = lax.broadcasted_iota(jnp.int32, weight_ref.shape, 0)
    masked = jnp.where(slot < count_ref[...], weight_ref[...], 0.0)
    for piece, slots_ref in enumerate(slots_refs):
        cut = slice(piece * LANES, (piece + 1) * LANES)
        slots_ref[...] = index_ref[:, cut]
        masked_ref[cut, :] = masked[:, cut].T
    leave.wait()


def prepare(ka, mix_wide, grad, index, weight, count, halo):
    channels, atoms = grad.shape
    slots = index.shape[0]
    per_side = halo.shape[1]
    own = atoms // lax.axis_size("ka")
    whole = pl.BlockSpec(memory_space=pltpu.VMEM)
    return pl.pallas_call(
        prepare_kernel,
        grid_spec=pltpu.PrefetchScalarGridSpec(
            num_scalar_prefetch=1,
            grid=(1,),
            in_specs=[
                pl.BlockSpec(memory_space=pltpu.SMEM),
                whole,
                whole,
                pl.BlockSpec((slots, own), lambda i, ka: (0, ka[0])),
                pl.BlockSpec((slots, own), lambda i, ka: (0, ka[0])),
                pl.BlockSpec((1, own), lambda i, ka: (0, ka[0])),
            ],
            out_specs=[pl.BlockSpec(memory_space=pltpu.HBM)] + [whole] * (2 + own // LANES),
            scratch_shapes=[
                pltpu.VMEM((2 * per_side, LANES), F32),
                pltpu.VMEM((atoms, LANES), F32),
                pltpu.SemaphoreType.DMA(()),
            ],
        ),
        out_shape=[
            pltpu.HBM((atoms + 2 * per_side, LANES), F32),
            jax.ShapeDtypeStruct((2 * per_side, LANES), BF16),
            jax.ShapeDtypeStruct((own, slots), F32),
        ]
        + [jax.ShapeDtypeStruct((slots, LANES), jnp.int32)] * (own // LANES),
        compiler_params=pltpu.CompilerParams(vmem_limit_bytes=12 << 20),
        cost_estimate=pl.CostEstimate(flops=1_000_000_000, bytes_accessed=8_000_000, transcendentals=0),
        name="prepare",
    )(ka, halo, mix_wide, grad, index, weight, count)


def short_kernel(index_ref, weight_ref, rows_ref, out_ref, sums_ref):
    sublane = lax.broadcasted_iota(jnp.int32, (8, LANES), 0)

    def group(g, carry):
        first = pl.multiple_of(g * 8, 8)
        weights = weight_ref[pl.ds(first, 8), :]
        total = jnp.zeros((8, LANES), F32)
        for s in range(weight_ref.shape[1]):
            picked = jnp.broadcast_to(rows_ref[index_ref[s * LANES + first]], (8, LANES))
            for a in range(1, 8):
                row = jnp.broadcast_to(rows_ref[index_ref[s * LANES + first + a]], (8, LANES))
                picked = jnp.where(sublane == a, row, picked)
            total = total + picked * weights[:, s : s + 1]
        sums_ref[pl.ds(first, 8), :] = total
        return carry

    lax.fori_loop(0, LANES // 8, group, 0)
    out_ref[...] = sums_ref[...].T[: out_ref.shape[0], :]


def short_sums(piece, channels, index, weight, rows):
    slots = weight.shape[1]
    return pl.pallas_call(
        short_kernel,
        grid=(1,),
        in_specs=[
            pl.BlockSpec(memory_space=pltpu.SMEM),
            pl.BlockSpec((LANES, slots), lambda i: (piece, 0)),
            pl.BlockSpec(memory_space=pltpu.VMEM),
        ],
        out_specs=pl.BlockSpec(memory_space=pltpu.VMEM),
        out_shape=jax.ShapeDtypeStruct((channels, LANES), F32),
        scratch_shapes=[pltpu.VMEM((LANES, LANES), F32)],
        compiler_params=pltpu.CompilerParams(vmem_limit_bytes=6 << 20),
        cost_estimate=pl.CostEstimate(flops=100_000_000, bytes_accessed=400_000, transcendentals=0),
        name="short_sums",
    )(index, weight, rows)


def local(
    grad_out,
    frac_pos,
    k_index,
    ewald_filter,
    struct_fac,
    out_weight,
    pair_mix,
    pair_weight,
    nbr_index,
    nbr_count,
    halo_send,
):
    channels, local_atoms = grad_out.shape
    ka_size, dom_size = lax.axis_size("ka"), lax.axis_size("dom")
    own_rows = local_atoms // ka_size
    k_count = k_index.shape[1]

    ka = lax.axis_index("ka").astype(jnp.int32)
    mix_wide = jnp.pad(pair_mix, ((0, LANES - channels), (0, 0)))
    rows, send, masked, *slots = prepare(
        ka[None],
        mix_wide,
        grad_out,
        pltpu.with_memory_space_constraint(nbr_index, pltpu.HBM),
        pltpu.with_memory_space_constraint(pair_weight, pltpu.HBM),
        nbr_count[None, :],
        halo_send,
    )
    per_side = halo_send.shape[1]
    from_left = shifted(send[:per_side], "dom", 1)
    from_right = shifted(send[per_side:], "dom", -1)
    short = []

    def short_piece():
        piece = len(short)
        short.append(short_sums(piece, channels, slots[piece].reshape(-1), masked, extended))

    def beside(value, bit, pieces):
        nonlocal slots
        value, slots = lax.optimization_barrier((value, slots))
        received = swapped(value, "dom", bit)
        start = len(short)
        for _ in range(pieces):
            short_piece()
        received, short[start:] = lax.optimization_barrier((received, short[start:]))
        return received.astype(F32)

    k_rows = k_index.astype(BF16).T
    k_triple = jnp.concatenate([k_rows, k_rows, k_rows, jnp.zeros((k_count, 7), BF16)], axis=1)
    frac_late, send_late = lax.optimization_barrier((frac_pos, send))
    q, table = front(out_weight, grad_out, frac_late, k_triple)
    q, from_left, from_right = lax.optimization_barrier((q, from_left, from_right))
    ghosts = jnp.concatenate([from_left, from_right], axis=0).astype(F32)
    extended = lax.dynamic_update_slice_in_dim(rows, ghosts, local_atoms, 0)
    extended = lax.optimization_barrier(extended)[:, None, :]

    half = channels // 2
    core = lax.axis_index("dom") % 2
    mine = lax.dynamic_slice_in_dim(q, core * half, half, 0)
    other = lax.dynamic_slice_in_dim(q, (1 - core) * half, half, 0)
    total = mine + beside(other.astype(BF16), 1, 0)
    bit = 2
    while bit < dom_size:
        rounded = total.astype(BF16)
        total = rounded.astype(F32) + beside(rounded, bit, 0 if bit == 8 else 1)
        bit *= 2
    partner = beside(total, 1, 0)
    q = jnp.where(
        core == 0,
        jnp.concatenate([total, partner], axis=0),
        jnp.concatenate([partner, total], axis=0),
    )
    q_cos, q_sin = q[:, :k_count], q[:, k_count:]
    atom_total = local_atoms * dom_size
    d_filter = (struct_fac[0] * q_cos + struct_fac[1] * q_sin) / atom_total
    p = jnp.concatenate([ewald_filter * q_cos, ewald_filter * q_sin], axis=1).astype(BF16)

    table = pltpu.with_memory_space_constraint(table, pltpu.HBM)
    parts = long_parts(p, table, ka_size)
    parts, slots = lax.optimization_barrier((parts, slots))
    parts = lax.all_to_all(parts, "ka", 0, 0, tiled=True)
    while len(short) < own_rows // LANES:
        short_piece()
    long_own = jnp.sum(parts.astype(F32), axis=0)
    own_grad = lax.dynamic_slice_in_dim(grad_out, ka * own_rows, own_rows, 1).astype(F32)
    d_feat = (own_grad + long_own + jnp.concatenate(short, axis=1)).astype(BF16)
    return (d_feat, d_filter)


def solution(mesh):
    return jax.shard_map(
        local,
        mesh=mesh,
        in_specs=(
            P(None, "dom"),
            P(None, "dom"),
            P(None, "ka"),
            P(None, "ka"),
            P(None, None, "ka"),
            P(),
            P(),
            P(None, "dom"),
            P(None, "dom"),
            P("dom"),
            P(None, "dom"),
        ),
        out_specs=(P(None, ("dom", "ka")), P(None, "ka")),
        check_vma=False,
    )
```

```python
import functools
import math

import jax
import jax.numpy as jnp
import numpy as np
from jax import lax
from jax.experimental import pallas as pl
from jax.experimental.pallas import tpu as pltpu
from jax.sharding import PartitionSpec as P

BF16 = jnp.bfloat16
F32 = jnp.float32
LANES = 128


def even_fit(function, terms):
    u = np.cos(np.pi * (np.arange(200) + 0.5) / 200) * 0.125 + 0.125
    fitted = np.polynomial.chebyshev.Chebyshev.fit(u, function(np.sqrt(u)), terms - 1, domain=[0, 0.25])
    return [float(c) for c in fitted.convert(kind=np.polynomial.Polynomial).coef]


SIN_HALF = even_fit(lambda r: math.sqrt(2) * np.sin(np.pi * r) / r, 4)
COS_HALF = even_fit(lambda r: math.sqrt(2) * np.cos(np.pi * r), 4)


def swapped(block, axis, bit):
    return lax.ppermute(block, axis, [(i, i ^ bit) for i in range(lax.axis_size(axis))])


def shifted(block, axis, distance):
    devices = range(lax.axis_size(axis))
    route = [((i - distance) % len(devices), i) for i in devices]
    return lax.ppermute(block, axis, route)


def front_kernel(
    rows, tile, mix_ref, grad_ref, frac_ref, k_ref,
    q_ref, whole_ref, pieces_ref, even_ref, odd_ref, held_ref, sems,
):
    step, last = pl.program_id(0), pl.num_programs(0) - 1
    slot = lax.rem(step, 2)
    table_ref = held_ref.at[slot]
    block = grad_ref.shape[1]
    k_count = k_ref.shape[0]
    turns_refs = (even_ref, odd_ref)

    def keep(at, slot):
        columns = pl.ds(pl.multiple_of(at * block, block), block)
        return pltpu.make_async_copy(held_ref.at[slot], whole_ref.at[:, columns], sems.at[slot])

    @pl.when(step == 0)
    def _():
        q_ref[...] = jnp.zeros_like(q_ref)
        pieces_ref[...] = jnp.zeros_like(pieces_ref)

    @pl.when(step >= 2)
    def _():
        keep(step - 2, slot).wait()

    frac = frac_ref[...]
    high = frac.astype(BF16).astype(F32)
    rest = frac - high
    middle = rest.astype(BF16).astype(F32)
    pieces_ref[0:3, :] = high
    pieces_ref[3:6, :] = middle
    pieces_ref[6:9, :] = rest - middle
    pieces = pieces_ref[...].astype(BF16)
    cot = jnp.dot(mix_ref[...], grad_ref[...], preferred_element_type=F32).astype(BF16)

    def turn(t):
        k_tile = k_ref[t * tile : (t + 1) * tile, :]
        turns_refs[t % 2][...] = jnp.dot(k_tile, pieces, preferred_element_type=F32)

    def fill(t):
        for row in range(0, tile, rows):
            turns = turns_refs[t % 2][row : row + rows, :]
            r = turns - jnp.round(turns)
            u = r * r
            s = SIN_HALF[-1]
            for coefficient in SIN_HALF[-2::-1]:
                s = s * u + coefficient
            s = s * r
            c = COS_HALF[-1]
            for coefficient in COS_HALF[-2::-1]:
                c = c * u + coefficient
            first = t * tile + row
            table_ref[first : first + rows, :] = (1.0 - s * s).astype(BF16)
            table_ref[k_count + first : k_count + first + rows, :] = (s * c).astype(BF16)

    def add(t):
        for first in (t * tile, k_count + t * tile):
            q_ref[:, first : first + tile] += lax.dot_general(
                cot, table_ref[first : first + tile, :], (((1,), (1,)), ((), ())),
                preferred_element_type=F32,
            )

    tiles = k_count // tile
    turn(0)
    for t in range(tiles):
        if t > 0:
            add(t - 1)
        if t + 1 < tiles:
            turn(t + 1)
        fill(t)
    add(tiles - 1)
    keep(step, slot).start()

    @pl.when(step == last)
    def _():
        keep(step - 1, 1 - slot).wait()
        keep(step, slot).wait()


def front(mix, grad, frac, k_triple, rows=16, tile=128, block=1024):
    channels, atoms = grad.shape
    k_count = k_triple.shape[0]
    return pl.pallas_call(
        functools.partial(front_kernel, rows, tile),
        grid=(atoms // block,),
        in_specs=[
            pl.BlockSpec((channels, channels), lambda i: (0, 0)),
            pl.BlockSpec((channels, block), lambda i: (0, i)),
            pl.BlockSpec((3, block), lambda i: (0, i)),
            pl.BlockSpec((k_count, 16), lambda i: (0, 0)),
        ],
        out_specs=[
            pl.BlockSpec((channels, 2 * k_count), lambda i: (0, 0)),
            pl.BlockSpec(memory_space=pltpu.HBM),
        ],
        out_shape=[
            jax.ShapeDtypeStruct((channels, 2 * k_count), F32),
            pltpu.HBM((2 * k_count, atoms), BF16),
        ],
        scratch_shapes=[
            pltpu.VMEM((16, block), F32),
            pltpu.VMEM((tile, block), F32),
            pltpu.VMEM((tile, block), F32),
            pltpu.VMEM((2, 2 * k_count, block), BF16),
            pltpu.SemaphoreType.DMA((2,)),
        ],
        compiler_params=pltpu.CompilerParams(vmem_limit_bytes=12 << 20),
        cost_estimate=pl.CostEstimate(flops=20_000_000_000, bytes_accessed=14_000_000, transcendentals=0),
        name="structure_sums",
    )(mix, grad, frac, k_triple)


def long_kernel(p_ref, table_ref, out_ref):
    parts, _, own = out_ref.shape
    for at in range(parts):
        out_ref[at] = jnp.dot(
            p_ref[...], table_ref[:, at * own : (at + 1) * own], preferred_element_type=F32
        ).astype(BF16)


def long_parts(p, table, parts):
    whole = pl.BlockSpec(memory_space=pltpu.VMEM)
    return pl.pallas_call(
        long_kernel,
        in_specs=[whole, whole],
        out_specs=whole,
        out_shape=jax.ShapeDtypeStruct((parts, p.shape[0], table.shape[1] // parts), BF16),
        compiler_params=pltpu.CompilerParams(vmem_limit_bytes=24 << 20),
        cost_estimate=pl.CostEstimate(flops=800_000_000, bytes_accessed=14_000_000, transcendentals=0),
        name="long_parts",
    )(p, table)


def prepare_kernel(
    ka_ref, halo_ref, mix_ref, grad_ref, index_ref, weight_ref, count_ref,
    rows_ref, send_ref, masked_ref, *refs,
):
    *slots_refs, picked_ref, held_ref, sem = refs
    atoms = grad_ref.shape[1]
    block = math.gcd(atoms, 512)
    sends, per_side = send_ref.shape[0], halo_ref.shape[1]

    def mix(i, carry):
        first = pl.multiple_of(i * block, block)
        mixed = lax.dot_general(
            grad_ref[:, pl.ds(first, block)], mix_ref[...], (((0,), (1,)), ((), ())),
            preferred_element_type=F32,
        )
        held_ref[pl.ds(first, block), :] = mixed.astype(BF16).astype(F32)
        return carry

    lax.fori_loop(0, atoms // block, mix, 0)
    leave = pltpu.make_async_copy(held_ref, rows_ref.at[pl.ds(0, atoms)], sem)
    leave.start()

    for side in range(2):
        def pick(i, carry, side=side):
            first = pl.multiple_of(i * 32, 32)
            for j in range(32):
                picked_ref[pl.ds(side * per_side + first + j, 1), :] = held_ref[
                    pl.ds(halo_ref[side, first + j], 1), :
                ]
            return carry

        lax.fori_loop(0, per_side // 32, pick, 0)
    send_ref[...] = picked_ref[...].astype(BF16)

    slot = lax.broadcasted_iota(jnp.int32, weight_ref.shape, 0)
    masked = jnp.where(slot < count_ref[...], weight_ref[...], 0.0)
    for piece, slots_ref in enumerate(slots_refs):
        cut = slice(piece * LANES, (piece + 1) * LANES)
        slots_ref[:, : index_ref.shape[0]] = index_ref[:, cut].T
        masked_ref[cut, :] = masked[:, cut].T
    leave.wait()


def prepare(ka, mix_wide, grad, index, weight, count, halo):
    channels, atoms = grad.shape
    slots = index.shape[0]
    per_side = halo.shape[1]
    own = atoms // lax.axis_size("ka")
    whole = pl.BlockSpec(memory_space=pltpu.VMEM)
    return pl.pallas_call(
        prepare_kernel,
        grid_spec=pltpu.PrefetchScalarGridSpec(
            num_scalar_prefetch=1,
            grid=(1,),
            in_specs=[
                pl.BlockSpec(memory_space=pltpu.SMEM),
                whole,
                whole,
                pl.BlockSpec((slots, own), lambda i, ka: (0, ka[0])),
                pl.BlockSpec((slots, own), lambda i, ka: (0, ka[0])),
                pl.BlockSpec((1, own), lambda i, ka: (0, ka[0])),
            ],
            out_specs=[pl.BlockSpec(memory_space=pltpu.HBM)] + [whole] * (2 + own // LANES),
            scratch_shapes=[
                pltpu.VMEM((2 * per_side, LANES), F32),
                pltpu.VMEM((atoms, LANES), F32),
                pltpu.SemaphoreType.DMA(()),
            ],
        ),
        out_shape=[
            pltpu.HBM((atoms + 2 * per_side, LANES), F32),
            jax.ShapeDtypeStruct((2 * per_side, LANES), BF16),
            jax.ShapeDtypeStruct((own, slots), F32),
        ]
        + [jax.ShapeDtypeStruct((LANES, LANES), jnp.int32)] * (own // LANES),
        compiler_params=pltpu.CompilerParams(vmem_limit_bytes=12 << 20),
        cost_estimate=pl.CostEstimate(flops=1_000_000_000, bytes_accessed=8_000_000, transcendentals=0),
        name="prepare",
    )(ka, halo, mix_wide, grad, index, weight, count)


def short_kernel(index_ref, weight_ref, rows_ref, out_ref, sums_ref, sems, *windows):
    sublane = lax.broadcasted_iota(jnp.int32, (8, LANES), 0)
    groups, depth = LANES // 8, len(windows)

    def fetch(g, w):
        block = index_ref.at[pl.ds(pl.multiple_of(g * 8, 8), 8)]
        return pltpu.make_async_copy(block, windows[w], sems.at[w])

    for w in range(depth):
        fetch(w, w).start()

    def round_of_groups(i, carry):
        for w in range(depth):
            g = i * depth + w
            fetch(g, w).wait()
            first = pl.multiple_of(g * 8, 8)
            weights = weight_ref[pl.ds(first, 8), :]
            total = jnp.zeros((8, LANES), F32)
            for s in range(weight_ref.shape[1]):
                picked = jnp.broadcast_to(rows_ref[windows[w][0, s]], (8, LANES))
                for a in range(1, 8):
                    row = jnp.broadcast_to(rows_ref[windows[w][a, s]], (8, LANES))
                    picked = jnp.where(sublane == a, row, picked)
                total = total + picked * weights[:, s : s + 1]
            sums_ref[pl.ds(first, 8), :] = total

            @pl.when(g + depth < groups)
            def _(g=g, w=w):
                fetch(g + depth, w).start()

        return carry

    lax.fori_loop(0, groups // depth, round_of_groups, 0)
    out_ref[...] = sums_ref[...].T[: out_ref.shape[0], :]


def short_sums(piece, channels, index, weight, rows, depth=4):
    slots = weight.shape[1]
    return pl.pallas_call(
        short_kernel,
        grid=(1,),
        in_specs=[
            pl.BlockSpec(memory_space=pltpu.VMEM),
            pl.BlockSpec((LANES, slots), lambda i: (piece, 0)),
            pl.BlockSpec(memory_space=pltpu.VMEM),
        ],
        out_specs=pl.BlockSpec(memory_space=pltpu.VMEM),
        out_shape=jax.ShapeDtypeStruct((channels, LANES), F32),
        scratch_shapes=[pltpu.VMEM((LANES, LANES), F32), pltpu.SemaphoreType.DMA((depth,))]
        + [pltpu.SMEM((8, LANES), jnp.int32)] * depth,
        compiler_params=pltpu.CompilerParams(vmem_limit_bytes=6 << 20),
        cost_estimate=pl.CostEstimate(flops=100_000_000, bytes_accessed=400_000, transcendentals=0),
        name="short_sums",
    )(index, weight, rows)


def local(
    grad_out,
    frac_pos,
    k_index,
    ewald_filter,
    struct_fac,
    out_weight,
    pair_mix,
    pair_weight,
    nbr_index,
    nbr_count,
    halo_send,
):
    channels, local_atoms = grad_out.shape
    ka_size, dom_size = lax.axis_size("ka"), lax.axis_size("dom")
    own_rows = local_atoms // ka_size
    k_count = k_index.shape[1]

    ka = lax.axis_index("ka").astype(jnp.int32)
    mix_wide = jnp.pad(pair_mix, ((0, LANES - channels), (0, 0)))
    rows, send, masked, *slots = prepare(
        ka[None],
        mix_wide,
        grad_out,
        pltpu.with_memory_space_constraint(nbr_index, pltpu.HBM),
        pltpu.with_memory_space_constraint(pair_weight, pltpu.HBM),
        nbr_count[None, :],
        halo_send,
    )
    per_side = halo_send.shape[1]
    from_left = shifted(send[:per_side], "dom", 1)
    from_right = shifted(send[per_side:], "dom", -1)
    short = []

    def short_piece():
        piece = len(short)
        short.append(short_sums(piece, channels, slots[piece], masked, extended))

    def beside(value, bit, pieces):
        nonlocal slots
        value, slots = lax.optimization_barrier((value, slots))
        received = swapped(value, "dom", bit)
        start = len(short)
        for _ in range(pieces):
            short_piece()
        received, short[start:] = lax.optimization_barrier((received, short[start:]))
        return received.astype(F32)

    k_rows = k_index.astype(BF16).T
    k_triple = jnp.concatenate([k_rows, k_rows, k_rows, jnp.zeros((k_count, 7), BF16)], axis=1)
    frac_late, send_late = lax.optimization_barrier((frac_pos, send))
    q, table = front(out_weight, grad_out, frac_late, k_triple)
    q, from_left, from_right = lax.optimization_barrier((q, from_left, from_right))
    ghosts = jnp.concatenate([from_left, from_right], axis=0).astype(F32)
    extended = lax.dynamic_update_slice_in_dim(rows, ghosts, local_atoms, 0)
    extended = lax.optimization_barrier(extended)[:, None, :]

    half = channels // 2
    core = lax.axis_index("dom") % 2
    mine = lax.dynamic_slice_in_dim(q, core * half, half, 0)
    other = lax.dynamic_slice_in_dim(q, (1 - core) * half, half, 0)
    total = mine + beside(other.astype(BF16), 1, 0)
    bit = 2
    while bit < dom_size:
        rounded = total.astype(BF16)
        total = rounded.astype(F32) + beside(rounded, bit, 0 if bit == 16 else 1)
        bit *= 2
    partner = beside(total, 1, 0)
    q = jnp.where(
        core == 0,
        jnp.concatenate([total, partner], axis=0),
        jnp.concatenate([partner, total], axis=0),
    )
    q_cos, q_sin = q[:, :k_count], q[:, k_count:]
    atom_total = local_atoms * dom_size
    d_filter = (struct_fac[0] * q_cos + struct_fac[1] * q_sin) / atom_total
    p = jnp.concatenate([ewald_filter * q_cos, ewald_filter * q_sin], axis=1).astype(BF16)

    parts = long_parts(p, table, ka_size)
    parts, slots = lax.optimization_barrier((parts, slots))
    parts = lax.all_to_all(parts, "ka", 0, 0, tiled=True)
    while len(short) < own_rows // LANES:
        short_piece()
    long_own = jnp.sum(parts.astype(F32), axis=0)
    own_grad = lax.dynamic_slice_in_dim(grad_out, ka * own_rows, own_rows, 1).astype(F32)
    d_feat = (own_grad + long_own + jnp.concatenate(short, axis=1)).astype(BF16)
    return (d_feat, d_filter)


def solution(mesh):
    return jax.shard_map(
        local,
        mesh=mesh,
        in_specs=(
            P(None, "dom"),
            P(None, "dom"),
            P(None, "ka"),
            P(None, "ka"),
            P(None, None, "ka"),
            P(),
            P(),
            P(None, "dom"),
            P(None, "dom"),
            P("dom"),
            P(None, "dom"),
        ),
        out_specs=(P(None, ("dom", "ka")), P(None, "ka")),
        check_vma=False,
    )
```

```python
import functools
import math

import jax
import jax.numpy as jnp
import numpy as np
from jax import lax
from jax.experimental import pallas as pl
from jax.experimental.pallas import tpu as pltpu
from jax.sharding import PartitionSpec as P

BF16 = jnp.bfloat16
F32 = jnp.float32
LANES = 128


def even_fit(function, terms):
    u = np.cos(np.pi * (np.arange(200) + 0.5) / 200) * 0.125 + 0.125
    fitted = np.polynomial.chebyshev.Chebyshev.fit(u, function(np.sqrt(u)), terms - 1, domain=[0, 0.25])
    return [float(c) for c in fitted.convert(kind=np.polynomial.Polynomial).coef]


SIN_HALF = even_fit(lambda r: math.sqrt(2) * np.sin(np.pi * r) / r, 4)
COS_HALF = even_fit(lambda r: math.sqrt(2) * np.cos(np.pi * r), 4)


def swapped(block, axis, bit):
    return lax.ppermute(block, axis, [(i, i ^ bit) for i in range(lax.axis_size(axis))])


def shifted(block, axis, distance):
    devices = range(lax.axis_size(axis))
    route = [((i - distance) % len(devices), i) for i in devices]
    return lax.ppermute(block, axis, route)


def front_kernel(
    rows, tile, mix_ref, grad_ref, frac_ref, k_ref,
    q_ref, whole_ref, pieces_ref, even_ref, odd_ref, held_ref, sems,
):
    step, last = pl.program_id(0), pl.num_programs(0) - 1
    slot = lax.rem(step, 2)
    table_ref = held_ref.at[slot]
    block = grad_ref.shape[1]
    k_count = k_ref.shape[0]
    turns_refs = (even_ref, odd_ref)

    def keep(at, slot):
        columns = pl.ds(pl.multiple_of(at * block, block), block)
        return pltpu.make_async_copy(held_ref.at[slot], whole_ref.at[:, columns], sems.at[slot])

    @pl.when(step == 0)
    def _():
        q_ref[...] = jnp.zeros_like(q_ref)
        pieces_ref[...] = jnp.zeros_like(pieces_ref)

    @pl.when(step >= 2)
    def _():
        keep(step - 2, slot).wait()

    frac = frac_ref[...]
    high = frac.astype(BF16).astype(F32)
    rest = frac - high
    middle = rest.astype(BF16).astype(F32)
    pieces_ref[0:3, :] = high
    pieces_ref[3:6, :] = middle
    pieces_ref[6:9, :] = rest - middle
    pieces = pieces_ref[...].astype(BF16)
    cot = jnp.dot(mix_ref[...], grad_ref[...], preferred_element_type=F32).astype(BF16)

    def turn(t):
        k_tile = k_ref[t * tile : (t + 1) * tile, :]
        turns_refs[t % 2][...] = jnp.dot(k_tile, pieces, preferred_element_type=F32)

    def fill(t):
        for row in range(0, tile, rows):
            turns = turns_refs[t % 2][row : row + rows, :]
            r = turns - jnp.round(turns)
            u = r * r
            s = SIN_HALF[-1]
            for coefficient in SIN_HALF[-2::-1]:
                s = s * u + coefficient
            s = s * r
            c = COS_HALF[-1]
            for coefficient in COS_HALF[-2::-1]:
                c = c * u + coefficient
            first = t * tile + row
            table_ref[first : first + rows, :] = (1.0 - s * s).astype(BF16)
            table_ref[k_count + first : k_count + first + rows, :] = (s * c).astype(BF16)

    def add(t):
        for first in (t * tile, k_count + t * tile):
            q_ref[:, first : first + tile] += lax.dot_general(
                cot, table_ref[first : first + tile, :], (((1,), (1,)), ((), ())),
                preferred_element_type=F32,
            )

    tiles = k_count // tile
    turn(0)
    for t in range(tiles):
        if t > 0:
            add(t - 1)
        if t + 1 < tiles:
            turn(t + 1)
        fill(t)
    add(tiles - 1)
    keep(step, slot).start()

    @pl.when(step == last)
    def _():
        keep(step - 1, 1 - slot).wait()
        keep(step, slot).wait()


def front(mix, grad, frac, k_triple, rows=16, tile=128, block=1024):
    channels, atoms = grad.shape
    k_count = k_triple.shape[0]
    return pl.pallas_call(
        functools.partial(front_kernel, rows, tile),
        grid=(atoms // block,),
        in_specs=[
            pl.BlockSpec((channels, channels), lambda i: (0, 0)),
            pl.BlockSpec((channels, block), lambda i: (0, i)),
            pl.BlockSpec((3, block), lambda i: (0, i)),
            pl.BlockSpec((k_count, 16), lambda i: (0, 0)),
        ],
        out_specs=[
            pl.BlockSpec((channels, 2 * k_count), lambda i: (0, 0)),
            pl.BlockSpec(memory_space=pltpu.HBM),
        ],
        out_shape=[
            jax.ShapeDtypeStruct((channels, 2 * k_count), F32),
            pltpu.HBM((2 * k_count, atoms), BF16),
        ],
        scratch_shapes=[
            pltpu.VMEM((16, block), F32),
            pltpu.VMEM((tile, block), F32),
            pltpu.VMEM((tile, block), F32),
            pltpu.VMEM((2, 2 * k_count, block), BF16),
            pltpu.SemaphoreType.DMA((2,)),
        ],
        compiler_params=pltpu.CompilerParams(vmem_limit_bytes=12 << 20),
        cost_estimate=pl.CostEstimate(flops=20_000_000_000, bytes_accessed=14_000_000, transcendentals=0),
        name="structure_sums",
    )(mix, grad, frac, k_triple)


def long_kernel(p_ref, table_ref, out_ref, held_ref, sems):
    parts, _, own = out_ref.shape
    fetches = [
        pltpu.make_async_copy(
            table_ref.at[:, at * own : (at + 1) * own], held_ref.at[at], sems.at[at]
        )
        for at in range(parts)
    ]
    for fetch in fetches:
        fetch.start()
    for at, fetch in enumerate(fetches):
        fetch.wait()
        out_ref[at] = jnp.dot(p_ref[...], held_ref[at], preferred_element_type=F32).astype(BF16)


def long_parts(p, table, parts):
    channels, depth = p.shape
    own = table.shape[1] // parts
    return pl.pallas_call(
        long_kernel,
        in_specs=[pl.BlockSpec(memory_space=pltpu.VMEM), pl.BlockSpec(memory_space=pltpu.HBM)],
        out_specs=pl.BlockSpec(memory_space=pltpu.VMEM),
        out_shape=jax.ShapeDtypeStruct((parts, channels, own), BF16),
        scratch_shapes=[pltpu.VMEM((parts, depth, own), BF16), pltpu.SemaphoreType.DMA((parts,))],
        compiler_params=pltpu.CompilerParams(vmem_limit_bytes=18 << 20),
        cost_estimate=pl.CostEstimate(flops=800_000_000, bytes_accessed=14_000_000, transcendentals=0),
        name="long_parts",
    )(p, pltpu.with_memory_space_constraint(table, pltpu.HBM))


def prepare_kernel(
    ka_ref, halo_ref, mix_ref, grad_ref, index_ref, weight_ref, count_ref,
    rows_ref, send_ref, masked_ref, *refs,
):
    *slots_refs, picked_ref, held_ref, wide_ref, sem = refs
    channels = mix_ref.shape[0]
    wide_ref[channels:, :] = jnp.zeros((LANES - channels, channels), BF16)
    wide_ref[:channels, :] = mix_ref[...]
    atoms = grad_ref.shape[1]
    block = math.gcd(atoms, 512)
    sends, per_side = send_ref.shape[0], halo_ref.shape[1]

    def mix(i, carry):
        first = pl.multiple_of(i * block, block)
        mixed = lax.dot_general(
            grad_ref[:, pl.ds(first, block)], wide_ref[...], (((0,), (1,)), ((), ())),
            preferred_element_type=F32,
        )
        held_ref[pl.ds(first, block), :] = mixed.astype(BF16).astype(F32)
        return carry

    lax.fori_loop(0, atoms // block, mix, 0)
    leave = pltpu.make_async_copy(held_ref, rows_ref.at[pl.ds(0, atoms)], sem)
    leave.start()

    for side in range(2):
        for j in range(per_side):
            picked_ref[side * per_side + j, :] = held_ref[halo_ref[side, j], :]
    send_ref[...] = picked_ref[...].astype(BF16)

    slot = lax.broadcasted_iota(jnp.int32, weight_ref.shape, 0)
    masked = jnp.where(slot < count_ref[...], weight_ref[...], 0.0)
    for piece, slots_ref in enumerate(slots_refs):
        cut = slice(piece * LANES, (piece + 1) * LANES)
        slots_ref[:, : index_ref.shape[0]] = index_ref[:, cut].T
        masked_ref[cut, :] = masked[:, cut].T
    leave.wait()


def prepare(ka, mix, grad, index, weight, count, halo):
    channels, atoms = grad.shape
    slots = index.shape[0]
    per_side = halo.shape[1]
    own = atoms // lax.axis_size("ka")
    whole = pl.BlockSpec(memory_space=pltpu.VMEM)
    return pl.pallas_call(
        prepare_kernel,
        grid_spec=pltpu.PrefetchScalarGridSpec(
            num_scalar_prefetch=1,
            grid=(1,),
            in_specs=[
                pl.BlockSpec(memory_space=pltpu.SMEM),
                whole,
                whole,
                pl.BlockSpec((slots, own), lambda i, ka: (0, ka[0])),
                pl.BlockSpec((slots, own), lambda i, ka: (0, ka[0])),
                pl.BlockSpec((1, own), lambda i, ka: (0, ka[0])),
            ],
            out_specs=[pl.BlockSpec(memory_space=pltpu.HBM)] + [whole] * (2 + own // LANES),
            scratch_shapes=[
                pltpu.VMEM((2 * per_side, LANES), F32),
                pltpu.VMEM((atoms, LANES), F32),
                pltpu.VMEM((LANES, channels), BF16),
                pltpu.SemaphoreType.DMA(()),
            ],
        ),
        out_shape=[
            pltpu.HBM((atoms + 2 * per_side, LANES), F32),
            jax.ShapeDtypeStruct((2 * per_side, LANES), BF16),
            jax.ShapeDtypeStruct((own, slots), F32),
        ]
        + [jax.ShapeDtypeStruct((LANES, LANES), jnp.int32)] * (own // LANES),
        compiler_params=pltpu.CompilerParams(vmem_limit_bytes=12 << 20),
        cost_estimate=pl.CostEstimate(flops=1_000_000_000, bytes_accessed=8_000_000, transcendentals=0),
        name="prepare",
    )(ka, halo, mix, grad, index, weight, count)


def short_kernel(index_ref, weight_ref, rows_ref, out_ref, sums_ref, sems, *windows):
    sublane = lax.broadcasted_iota(jnp.int32, (8, LANES), 0)
    groups, depth = LANES // 8, len(windows)

    def fetch(g, w):
        block = index_ref.at[pl.ds(pl.multiple_of(g * 8, 8), 8)]
        return pltpu.make_async_copy(block, windows[w], sems.at[w])

    for w in range(depth):
        fetch(w, w).start()

    def round_of_groups(i, carry):
        for w in range(depth):
            g = i * depth + w
            fetch(g, w).wait()
            first = pl.multiple_of(g * 8, 8)
            weights = weight_ref[pl.ds(first, 8), :]
            total = jnp.zeros((8, LANES), F32)
            for s in range(weight_ref.shape[1]):
                picked = jnp.broadcast_to(rows_ref[windows[w][0, s]], (8, LANES))
                for a in range(1, 8):
                    row = jnp.broadcast_to(rows_ref[windows[w][a, s]], (8, LANES))
                    picked = jnp.where(sublane == a, row, picked)
                total = total + picked * weights[:, s : s + 1]
            sums_ref[pl.ds(first, 8), :] = total

            @pl.when(g + depth < groups)
            def _(g=g, w=w):
                fetch(g + depth, w).start()

        return carry

    lax.fori_loop(0, groups // depth, round_of_groups, 0)
    out_ref[...] = sums_ref[...].T[: out_ref.shape[0], :]


def short_sums(piece, channels, index, weight, rows, flops, depth=4):
    slots = weight.shape[1]
    return pl.pallas_call(
        short_kernel,
        grid=(1,),
        in_specs=[
            pl.BlockSpec(memory_space=pltpu.VMEM),
            pl.BlockSpec((LANES, slots), lambda i: (piece, 0)),
            pl.BlockSpec(memory_space=pltpu.VMEM),
        ],
        out_specs=pl.BlockSpec(memory_space=pltpu.VMEM),
        out_shape=jax.ShapeDtypeStruct((channels, LANES), F32),
        scratch_shapes=[pltpu.VMEM((LANES, LANES), F32), pltpu.SemaphoreType.DMA((depth,))]
        + [pltpu.SMEM((8, LANES), jnp.int32)] * depth,
        compiler_params=pltpu.CompilerParams(vmem_limit_bytes=6 << 20),
        cost_estimate=pl.CostEstimate(flops=flops, bytes_accessed=400_000, transcendentals=0),
        name="short_sums",
    )(index, weight, rows)


def local(
    grad_out,
    frac_pos,
    k_index,
    ewald_filter,
    struct_fac,
    out_weight,
    pair_mix,
    pair_weight,
    nbr_index,
    nbr_count,
    halo_send,
):
    channels, local_atoms = grad_out.shape
    ka_size, dom_size = lax.axis_size("ka"), lax.axis_size("dom")
    own_rows = local_atoms // ka_size
    k_count = k_index.shape[1]

    ka = lax.axis_index("ka").astype(jnp.int32)
    rows, send, masked, *slots = prepare(
        ka[None],
        pair_mix,
        *(
            pltpu.with_memory_space_constraint(a, pltpu.HBM)
            for a in (grad_out, nbr_index, pair_weight, nbr_count[None, :], halo_send)
        ),
    )
    per_side = halo_send.shape[1]
    from_left = shifted(send[:per_side], "dom", 1)
    from_right = shifted(send[per_side:], "dom", -1)
    short = []

    def short_piece(flops):
        piece = len(short)
        short.append(short_sums(piece, channels, slots[piece], masked, extended, flops))

    def beside(value, bit, pieces):
        nonlocal slots
        value, slots = lax.optimization_barrier((value, slots))
        received = swapped(value, "dom", bit)
        start = len(short)
        for _ in range(pieces):
            short_piece(4_000_000_000)
        received, short[start:] = lax.optimization_barrier((received, short[start:]))
        return received.astype(F32)

    k_rows = k_index.astype(BF16).T
    k_triple = jnp.concatenate([k_rows, k_rows, k_rows, jnp.zeros((k_count, 7), BF16)], axis=1)
    frac_late, send_late = lax.optimization_barrier((frac_pos, send))
    q, table = front(out_weight, grad_out, frac_late, k_triple)
    q, from_left, from_right = lax.optimization_barrier((q, from_left, from_right))
    ghosts = jnp.concatenate([from_left, from_right], axis=0).astype(F32)
    extended = lax.dynamic_update_slice_in_dim(rows, ghosts, local_atoms, 0)
    extended = lax.optimization_barrier(extended)[:, None, :]

    half = channels // 2
    core = lax.axis_index("dom") % 2
    mine = lax.dynamic_slice_in_dim(q, core * half, half, 0)
    other = lax.dynamic_slice_in_dim(q, (1 - core) * half, half, 0)
    total = mine + beside(other.astype(BF16), 1, 0)
    bit = 2
    while bit < dom_size:
        rounded = total.astype(BF16)
        total = rounded.astype(F32) + beside(rounded, bit, 0 if bit == 2 else 1)
        bit *= 2
    partner = beside(total, 1, 0)
    q = jnp.where(
        core == 0,
        jnp.concatenate([total, partner], axis=0),
        jnp.concatenate([partner, total], axis=0),
    )
    q_cos, q_sin = q[:, :k_count], q[:, k_count:]
    atom_total = local_atoms * dom_size
    d_filter = (struct_fac[0] * q_cos + struct_fac[1] * q_sin) / atom_total
    p = jnp.concatenate([ewald_filter * q_cos, ewald_filter * q_sin], axis=1).astype(BF16)

    parts = long_parts(p, table, ka_size)
    parts, slots = lax.optimization_barrier((parts, slots))
    parts = lax.all_to_all(parts, "ka", 0, 0, tiled=True)
    while len(short) < own_rows // LANES:
        short_piece(100_000_000)
    long_own = jnp.sum(parts.astype(F32), axis=0)
    own_grad = lax.dynamic_slice_in_dim(grad_out, ka * own_rows, own_rows, 1).astype(F32)
    d_feat = (own_grad + long_own + jnp.concatenate(short, axis=1)).astype(BF16)
    return (d_feat, d_filter)


def solution(mesh):
    return jax.shard_map(
        local,
        mesh=mesh,
        in_specs=(
            P(None, "dom"),
            P(None, "dom"),
            P(None, "ka"),
            P(None, "ka"),
            P(None, None, "ka"),
            P(),
            P(),
            P(None, "dom"),
            P(None, "dom"),
            P("dom"),
            P(None, "dom"),
        ),
        out_specs=(P(None, ("dom", "ka")), P(None, "ka")),
        check_vma=False,
    )
```

```python
import functools
import math

import jax
import jax.numpy as jnp
import numpy as np
from jax import lax
from jax.experimental import pallas as pl
from jax.experimental.pallas import tpu as pltpu
from jax.sharding import PartitionSpec as P

BF16 = jnp.bfloat16
F32 = jnp.float32
LANES = 128


def even_fit(function, terms):
    u = np.cos(np.pi * (np.arange(200) + 0.5) / 200) * 0.125 + 0.125
    fitted = np.polynomial.chebyshev.Chebyshev.fit(u, function(np.sqrt(u)), terms - 1, domain=[0, 0.25])
    return [float(c) for c in fitted.convert(kind=np.polynomial.Polynomial).coef]


SIN_HALF = even_fit(lambda r: math.sqrt(2) * np.sin(np.pi * r) / r, 3)
COS_HALF = even_fit(lambda r: math.sqrt(2) * np.cos(np.pi * r), 4)


def swapped(block, axis, bit):
    return lax.ppermute(block, axis, [(i, i ^ bit) for i in range(lax.axis_size(axis))])


def shifted(block, axis, distance):
    devices = range(lax.axis_size(axis))
    route = [((i - distance) % len(devices), i) for i in devices]
    return lax.ppermute(block, axis, route)


def front_kernel(
    rows, tile, mix_ref, grad_ref, frac_ref, k_ref,
    q_ref, whole_ref, pieces_ref, even_ref, odd_ref, held_ref, sems,
):
    step, last = pl.program_id(0), pl.num_programs(0) - 1
    slot = lax.rem(step, 2)
    table_ref = held_ref.at[slot]
    block = grad_ref.shape[1]
    k_count = k_ref.shape[0]
    turns_refs = (even_ref, odd_ref)

    def keep(at, slot):
        columns = pl.ds(pl.multiple_of(at * block, block), block)
        return pltpu.make_async_copy(held_ref.at[slot], whole_ref.at[:, columns], sems.at[slot])

    @pl.when(step == 0)
    def _():
        q_ref[...] = jnp.zeros_like(q_ref)
        pieces_ref[...] = jnp.zeros_like(pieces_ref)

    @pl.when(step >= 2)
    def _():
        keep(step - 2, slot).wait()

    frac = frac_ref[...]
    high = frac.astype(BF16).astype(F32)
    rest = frac - high
    middle = rest.astype(BF16).astype(F32)
    pieces_ref[0:3, :] = high
    pieces_ref[3:6, :] = middle
    pieces_ref[6:9, :] = rest - middle
    pieces = pieces_ref[...].astype(BF16)
    cot = jnp.dot(mix_ref[...], grad_ref[...], preferred_element_type=F32).astype(BF16)

    def turn(t):
        k_tile = k_ref[t * tile : (t + 1) * tile, :]
        turns_refs[t % 2][...] = jnp.dot(k_tile, pieces, preferred_element_type=F32)

    def fill(t):
        for row in range(0, tile, rows):
            turns = turns_refs[t % 2][row : row + rows, :]
            r = turns - jnp.round(turns)
            u = r * r
            s = SIN_HALF[-1]
            for coefficient in SIN_HALF[-2::-1]:
                s = s * u + coefficient
            s = s * r
            c = COS_HALF[-1]
            for coefficient in COS_HALF[-2::-1]:
                c = c * u + coefficient
            first = t * tile + row
            table_ref[first : first + rows, :] = (1.0 - s * s).astype(BF16)
            table_ref[k_count + first : k_count + first + rows, :] = (s * c).astype(BF16)

    def add(t):
        for first in (t * tile, k_count + t * tile):
            q_ref[:, first : first + tile] += lax.dot_general(
                cot, table_ref[first : first + tile, :], (((1,), (1,)), ((), ())),
                preferred_element_type=F32,
            )

    tiles = k_count // tile
    turn(0)
    for t in range(tiles):
        if t > 0:
            add(t - 1)
        if t + 1 < tiles:
            turn(t + 1)
        fill(t)
    add(tiles - 1)
    keep(step, slot).start()

    @pl.when(step == last)
    def _():
        keep(step - 1, 1 - slot).wait()
        keep(step, slot).wait()


def front(mix, grad, frac, k_triple, rows=16, tile=128, block=1024):
    channels, atoms = grad.shape
    k_count = k_triple.shape[0]
    return pl.pallas_call(
        functools.partial(front_kernel, rows, tile),
        grid=(atoms // block,),
        in_specs=[
            pl.BlockSpec((channels, channels), lambda i: (0, 0)),
            pl.BlockSpec((channels, block), lambda i: (0, i)),
            pl.BlockSpec((3, block), lambda i: (0, i)),
            pl.BlockSpec((k_count, 16), lambda i: (0, 0)),
        ],
        out_specs=[
            pl.BlockSpec((channels, 2 * k_count), lambda i: (0, 0)),
            pl.BlockSpec(memory_space=pltpu.HBM),
        ],
        out_shape=[
            jax.ShapeDtypeStruct((channels, 2 * k_count), F32),
            pltpu.HBM((2 * k_count, atoms), BF16),
        ],
        scratch_shapes=[
            pltpu.VMEM((16, block), F32),
            pltpu.VMEM((tile, block), F32),
            pltpu.VMEM((tile, block), F32),
            pltpu.VMEM((2, 2 * k_count, block), BF16),
            pltpu.SemaphoreType.DMA((2,)),
        ],
        compiler_params=pltpu.CompilerParams(vmem_limit_bytes=12 << 20),
        cost_estimate=pl.CostEstimate(flops=20_000_000_000, bytes_accessed=14_000_000, transcendentals=0),
        name="structure_sums",
    )(mix, grad, frac, k_triple)


def long_kernel(p_ref, table_ref, out_ref, held_ref, sems):
    parts, _, own = out_ref.shape
    fetches = [
        pltpu.make_async_copy(
            table_ref.at[:, at * own : (at + 1) * own], held_ref.at[at], sems.at[at]
        )
        for at in range(parts)
    ]
    for fetch in fetches:
        fetch.start()
    for at, fetch in enumerate(fetches):
        fetch.wait()
        out_ref[at] = jnp.dot(p_ref[...], held_ref[at], preferred_element_type=F32).astype(BF16)


def long_parts(p, table, parts):
    channels, depth = p.shape
    own = table.shape[1] // parts
    return pl.pallas_call(
        long_kernel,
        in_specs=[pl.BlockSpec(memory_space=pltpu.VMEM), pl.BlockSpec(memory_space=pltpu.HBM)],
        out_specs=pl.BlockSpec(memory_space=pltpu.VMEM),
        out_shape=jax.ShapeDtypeStruct((parts, channels, own), BF16),
        scratch_shapes=[pltpu.VMEM((parts, depth, own), BF16), pltpu.SemaphoreType.DMA((parts,))],
        compiler_params=pltpu.CompilerParams(vmem_limit_bytes=18 << 20),
        cost_estimate=pl.CostEstimate(flops=800_000_000, bytes_accessed=14_000_000, transcendentals=0),
        name="long_parts",
    )(p, pltpu.with_memory_space_constraint(table, pltpu.HBM))


def prepare_kernel(
    ka_ref, halo_ref, mix_ref, grad_ref, index_ref, weight_ref, count_ref,
    rows_ref, send_ref, masked_ref, *refs,
):
    *slots_refs, picked_ref, held_ref, wide_ref, sem = refs
    channels = mix_ref.shape[0]
    wide_ref[channels:, :] = jnp.zeros((LANES - channels, channels), BF16)
    wide_ref[:channels, :] = mix_ref[...]
    atoms = grad_ref.shape[1]
    block = math.gcd(atoms, 512)
    sends, per_side = send_ref.shape[0], halo_ref.shape[1]

    def mix(i, carry):
        first = pl.multiple_of(i * block, block)
        mixed = lax.dot_general(
            grad_ref[:, pl.ds(first, block)], wide_ref[...], (((0,), (1,)), ((), ())),
            preferred_element_type=F32,
        )
        held_ref[pl.ds(first, block), :] = mixed.astype(BF16).astype(F32)
        return carry

    lax.fori_loop(0, atoms // block, mix, 0)
    leave = pltpu.make_async_copy(held_ref, rows_ref.at[pl.ds(0, atoms)], sem)
    leave.start()

    for side in range(2):
        for j in range(per_side):
            picked_ref[side * per_side + j, :] = held_ref[halo_ref[side, j], :]
    send_ref[...] = picked_ref[...].astype(BF16)

    slot = lax.broadcasted_iota(jnp.int32, weight_ref.shape, 0)
    masked = jnp.where(slot < count_ref[...], weight_ref[...], 0.0)
    for piece, slots_ref in enumerate(slots_refs):
        cut = slice(piece * LANES, (piece + 1) * LANES)
        slots_ref[:, : index_ref.shape[0]] = index_ref[:, cut].T
        masked_ref[cut, :] = masked[:, cut].T
    leave.wait()


def prepare(ka, mix, grad, index, weight, count, halo):
    channels, atoms = grad.shape
    slots = index.shape[0]
    per_side = halo.shape[1]
    own = atoms // lax.axis_size("ka")
    whole = pl.BlockSpec(memory_space=pltpu.VMEM)
    return pl.pallas_call(
        prepare_kernel,
        grid_spec=pltpu.PrefetchScalarGridSpec(
            num_scalar_prefetch=1,
            grid=(1,),
            in_specs=[
                pl.BlockSpec(memory_space=pltpu.SMEM),
                whole,
                whole,
                pl.BlockSpec((slots, own), lambda i, ka: (0, ka[0])),
                pl.BlockSpec((slots, own), lambda i, ka: (0, ka[0])),
                pl.BlockSpec((1, own), lambda i, ka: (0, ka[0])),
            ],
            out_specs=[pl.BlockSpec(memory_space=pltpu.HBM)] + [whole] * (2 + own // LANES),
            scratch_shapes=[
                pltpu.VMEM((2 * per_side, LANES), F32),
                pltpu.VMEM((atoms, LANES), F32),
                pltpu.VMEM((LANES, channels), BF16),
                pltpu.SemaphoreType.DMA(()),
            ],
        ),
        out_shape=[
            pltpu.HBM((atoms + 2 * per_side, LANES), F32),
            jax.ShapeDtypeStruct((2 * per_side, LANES), BF16),
            jax.ShapeDtypeStruct((own, slots), F32),
        ]
        + [jax.ShapeDtypeStruct((LANES, LANES), jnp.int32)] * (own // LANES),
        compiler_params=pltpu.CompilerParams(vmem_limit_bytes=12 << 20),
        cost_estimate=pl.CostEstimate(flops=1_000_000_000, bytes_accessed=8_000_000, transcendentals=0),
        name="prepare",
    )(ka, halo, mix, grad, index, weight, count)


def short_kernel(index_ref, weight_ref, rows_ref, out_ref, sums_ref, sems, *windows):
    sublane = lax.broadcasted_iota(jnp.int32, (8, LANES), 0)
    groups, depth = LANES // 8, len(windows)

    def fetch(g, w):
        block = index_ref.at[pl.ds(pl.multiple_of(g * 8, 8), 8)]
        return pltpu.make_async_copy(block, windows[w], sems.at[w])

    for w in range(depth):
        fetch(w, w).start()

    def round_of_groups(i, carry):
        for w in range(depth):
            g = i * depth + w
            fetch(g, w).wait()
            first = pl.multiple_of(g * 8, 8)
            weights = weight_ref[pl.ds(first, 8), :]
            total = jnp.zeros((8, LANES), F32)
            for s in range(weight_ref.shape[1]):
                picked = jnp.broadcast_to(rows_ref[windows[w][0, s]], (8, LANES))
                for a in range(1, 8):
                    row = jnp.broadcast_to(rows_ref[windows[w][a, s]], (8, LANES))
                    picked = jnp.where(sublane == a, row, picked)
                total = total + picked * weights[:, s : s + 1]
            sums_ref[pl.ds(first, 8), :] = total

            @pl.when(g + depth < groups)
            def _(g=g, w=w):
                fetch(g + depth, w).start()

        return carry

    lax.fori_loop(0, groups // depth, round_of_groups, 0)
    out_ref[...] = sums_ref[...].T[: out_ref.shape[0], :]


def short_sums(piece, channels, index, weight, rows, flops, depth=4):
    slots = weight.shape[1]
    return pl.pallas_call(
        short_kernel,
        grid=(1,),
        in_specs=[
            pl.BlockSpec(memory_space=pltpu.VMEM),
            pl.BlockSpec((LANES, slots), lambda i: (piece, 0)),
            pl.BlockSpec(memory_space=pltpu.VMEM),
        ],
        out_specs=pl.BlockSpec(memory_space=pltpu.VMEM),
        out_shape=jax.ShapeDtypeStruct((channels, LANES), F32),
        scratch_shapes=[pltpu.VMEM((LANES, LANES), F32), pltpu.SemaphoreType.DMA((depth,))]
        + [pltpu.SMEM((8, LANES), jnp.int32)] * depth,
        compiler_params=pltpu.CompilerParams(vmem_limit_bytes=6 << 20),
        cost_estimate=pl.CostEstimate(flops=flops, bytes_accessed=400_000, transcendentals=0),
        name="short_sums",
    )(index, weight, rows)


def near_kernel(index_ref, rows_ref, out_ref):
    out_ref[...] = index_ref[...]


def near(index, rows):
    return pl.pallas_call(
        near_kernel,
        in_specs=[pl.BlockSpec(memory_space=pltpu.VMEM)] * 2,
        out_specs=pl.BlockSpec(memory_space=pltpu.VMEM),
        out_shape=jax.ShapeDtypeStruct(index.shape, index.dtype),
        compiler_params=pltpu.CompilerParams(vmem_limit_bytes=6 << 20),
        cost_estimate=pl.CostEstimate(flops=1_000_000_000, bytes_accessed=400_000, transcendentals=0),
        name="near",
    )(index, rows)


def local(
    grad_out,
    frac_pos,
    k_index,
    ewald_filter,
    struct_fac,
    out_weight,
    pair_mix,
    pair_weight,
    nbr_index,
    nbr_count,
    halo_send,
):
    channels, local_atoms = grad_out.shape
    ka_size, dom_size = lax.axis_size("ka"), lax.axis_size("dom")
    own_rows = local_atoms // ka_size
    k_count = k_index.shape[1]

    ka = lax.axis_index("ka").astype(jnp.int32)
    rows, send, masked, *slots = prepare(
        ka[None],
        pair_mix,
        *(
            pltpu.with_memory_space_constraint(a, pltpu.HBM)
            for a in (grad_out, nbr_index, pair_weight, nbr_count[None, :], halo_send)
        ),
    )
    per_side = halo_send.shape[1]
    from_left = shifted(send[:per_side], "dom", 1)
    from_right = shifted(send[per_side:], "dom", -1)
    short = []

    def short_piece(flops):
        piece = len(short)
        short.append(short_sums(piece, channels, slots[piece], masked, extended, flops))

    def beside(value, bit, pieces):
        nonlocal slots
        value, slots = lax.optimization_barrier((value, slots))
        received = swapped(value, "dom", bit)
        start = len(short)
        if not pieces and bit == 2:
            slots[0] = near(slots[0], extended)
            received, slots[0] = lax.optimization_barrier((received, slots[0]))
        for _ in range(pieces):
            short_piece(4_000_000_000)
        received, short[start:] = lax.optimization_barrier((received, short[start:]))
        return received.astype(F32)

    k_rows = k_index.astype(BF16).T
    k_triple = jnp.concatenate([k_rows, k_rows, k_rows, jnp.zeros((k_count, 7), BF16)], axis=1)
    frac_late, send_late = lax.optimization_barrier((frac_pos, send))
    q, table = front(out_weight, grad_out, frac_late, k_triple)
    q, from_left, from_right = lax.optimization_barrier((q, from_left, from_right))
    ghosts = jnp.concatenate([from_left, from_right], axis=0).astype(F32)
    extended = lax.dynamic_update_slice_in_dim(rows, ghosts, local_atoms, 0)
    extended = lax.optimization_barrier(extended)[:, None, :]

    half = channels // 2
    core = lax.axis_index("dom") % 2
    mine = lax.dynamic_slice_in_dim(q, core * half, half, 0)
    other = lax.dynamic_slice_in_dim(q, (1 - core) * half, half, 0)
    total = mine + beside(other.astype(BF16), 1, 0)
    bit = 2
    while bit < dom_size:
        rounded = total.astype(BF16)
        total = rounded.astype(F32) + beside(rounded, bit, 0 if bit == 2 else 1)
        bit *= 2
    partner = beside(total, 1, 0)
    q = jnp.where(
        core == 0,
        jnp.concatenate([total, partner], axis=0),
        jnp.concatenate([partner, total], axis=0),
    )
    q_cos, q_sin = q[:, :k_count], q[:, k_count:]
    atom_total = local_atoms * dom_size
    d_filter = (struct_fac[0] * q_cos + struct_fac[1] * q_sin) / atom_total
    p = jnp.concatenate([ewald_filter * q_cos, ewald_filter * q_sin], axis=1).astype(BF16)

    parts = long_parts(p, table, ka_size)
    parts, slots = lax.optimization_barrier((parts, slots))
    parts = lax.all_to_all(parts, "ka", 0, 0, tiled=True)
    while len(short) < own_rows // LANES:
        short_piece(100_000_000)
    long_own = jnp.sum(parts.astype(F32), axis=0)
    own_grad = lax.dynamic_slice_in_dim(grad_out, ka * own_rows, own_rows, 1).astype(F32)
    d_feat = (own_grad + long_own + jnp.concatenate(short, axis=1)).astype(BF16)
    return (d_feat, d_filter)


def solution(mesh):
    return jax.shard_map(
        local,
        mesh=mesh,
        in_specs=(
            P(None, "dom"),
            P(None, "dom"),
            P(None, "ka"),
            P(None, "ka"),
            P(None, None, "ka"),
            P(),
            P(),
            P(None, "dom"),
            P(None, "dom"),
            P("dom"),
            P(None, "dom"),
        ),
        out_specs=(P(None, ("dom", "ka")), P(None, "ka")),
        check_vma=False,
    )
```

```python
import functools
import math

import jax
import jax.numpy as jnp
import numpy as np
from jax import lax
from jax.experimental import pallas as pl
from jax.experimental.pallas import tpu as pltpu
from jax.sharding import PartitionSpec as P

BF16 = jnp.bfloat16
F32 = jnp.float32
LANES = 128


def even_fit(function, terms):
    u = np.cos(np.pi * (np.arange(200) + 0.5) / 200) * 0.125 + 0.125
    fitted = np.polynomial.chebyshev.Chebyshev.fit(u, function(np.sqrt(u)), terms - 1, domain=[0, 0.25])
    return [float(c) for c in fitted.convert(kind=np.polynomial.Polynomial).coef]


SIN_HALF = even_fit(lambda r: math.sqrt(2) * np.sin(np.pi * r) / r, 3)
COS_HALF = even_fit(lambda r: math.sqrt(2) * np.cos(np.pi * r), 4)


def swapped(block, axis, bit):
    return lax.ppermute(block, axis, [(i, i ^ bit) for i in range(lax.axis_size(axis))])


def shifted(block, axis, distance):
    devices = range(lax.axis_size(axis))
    route = [((i - distance) % len(devices), i) for i in devices]
    return lax.ppermute(block, axis, route)


def front_kernel(
    rows, tile, mix_ref, grad_ref, frac_ref, k_ref,
    q_ref, whole_ref, pieces_ref, even_ref, odd_ref, held_ref, sems,
):
    step, last = pl.program_id(0), pl.num_programs(0) - 1
    slot = lax.rem(step, 2)
    table_ref = held_ref.at[slot]
    block = grad_ref.shape[1]
    k_count = k_ref.shape[0]
    turns_refs = (even_ref, odd_ref)

    def keep(at, slot):
        columns = pl.ds(pl.multiple_of(at * block, block), block)
        return pltpu.make_async_copy(held_ref.at[slot], whole_ref.at[:, columns], sems.at[slot])

    @pl.when(step == 0)
    def _():
        q_ref[...] = jnp.zeros_like(q_ref)
        pieces_ref[...] = jnp.zeros_like(pieces_ref)

    @pl.when(step >= 2)
    def _():
        keep(step - 2, slot).wait()

    frac = frac_ref[...]
    high = frac.astype(BF16).astype(F32)
    rest = frac - high
    middle = rest.astype(BF16).astype(F32)
    pieces_ref[0:3, :] = high
    pieces_ref[3:6, :] = middle
    pieces_ref[6:9, :] = rest - middle
    pieces = pieces_ref[...].astype(BF16)
    cot = jnp.dot(mix_ref[...], grad_ref[...], preferred_element_type=F32).astype(BF16)

    def turn(t):
        k_tile = k_ref[t * tile : (t + 1) * tile, :]
        turns_refs[t % 2][...] = jnp.dot(k_tile, pieces, preferred_element_type=F32)

    def fill(t):
        for row in range(0, tile, rows):
            turns = turns_refs[t % 2][row : row + rows, :]
            r = turns - jnp.round(turns)
            u = r * r
            s = SIN_HALF[-1]
            for coefficient in SIN_HALF[-2::-1]:
                s = s * u + coefficient
            s = s * r
            c = COS_HALF[-1]
            for coefficient in COS_HALF[-2::-1]:
                c = c * u + coefficient
            first = t * tile + row
            table_ref[first : first + rows, :] = (1.0 - s * s).astype(BF16)
            table_ref[k_count + first : k_count + first + rows, :] = (s * c).astype(BF16)

    def add(t):
        for first in (t * tile, k_count + t * tile):
            q_ref[:, first : first + tile] += lax.dot_general(
                cot, table_ref[first : first + tile, :], (((1,), (1,)), ((), ())),
                preferred_element_type=F32,
            )

    tiles = k_count // tile
    turn(0)
    for t in range(tiles):
        if t > 0:
            add(t - 1)
        if t + 1 < tiles:
            turn(t + 1)
        fill(t)
    add(tiles - 1)
    keep(step, slot).start()

    @pl.when(step == last)
    def _():
        keep(step - 1, 1 - slot).wait()
        keep(step, slot).wait()


def front(mix, grad, frac, k_triple, rows=16, tile=128, block=1024):
    channels, atoms = grad.shape
    k_count = k_triple.shape[0]
    return pl.pallas_call(
        functools.partial(front_kernel, rows, tile),
        grid=(atoms // block,),
        in_specs=[
            pl.BlockSpec((channels, channels), lambda i: (0, 0)),
            pl.BlockSpec((channels, block), lambda i: (0, i)),
            pl.BlockSpec((3, block), lambda i: (0, i)),
            pl.BlockSpec((k_count, 16), lambda i: (0, 0)),
        ],
        out_specs=[
            pl.BlockSpec((channels, 2 * k_count), lambda i: (0, 0)),
            pl.BlockSpec(memory_space=pltpu.HBM),
        ],
        out_shape=[
            jax.ShapeDtypeStruct((channels, 2 * k_count), F32),
            pltpu.HBM((2 * k_count, atoms), BF16),
        ],
        scratch_shapes=[
            pltpu.VMEM((16, block), F32),
            pltpu.VMEM((tile, block), F32),
            pltpu.VMEM((tile, block), F32),
            pltpu.VMEM((2, 2 * k_count, block), BF16),
            pltpu.SemaphoreType.DMA((2,)),
        ],
        compiler_params=pltpu.CompilerParams(vmem_limit_bytes=12 << 20),
        cost_estimate=pl.CostEstimate(flops=20_000_000_000, bytes_accessed=14_000_000, transcendentals=0),
        name="structure_sums",
    )(mix, grad, frac, k_triple)


def long_kernel(p_ref, table_ref, out_ref, held_ref, sems):
    parts, _, own = out_ref.shape
    fetches = [
        pltpu.make_async_copy(
            table_ref.at[:, at * own : (at + 1) * own], held_ref.at[at], sems.at[at]
        )
        for at in range(parts)
    ]
    for fetch in fetches:
        fetch.start()
    for at, fetch in enumerate(fetches):
        fetch.wait()
        out_ref[at] = jnp.dot(p_ref[...], held_ref[at], preferred_element_type=F32).astype(BF16)


def long_parts(p, table, parts):
    channels, depth = p.shape
    own = table.shape[1] // parts
    return pl.pallas_call(
        long_kernel,
        in_specs=[pl.BlockSpec(memory_space=pltpu.VMEM), pl.BlockSpec(memory_space=pltpu.HBM)],
        out_specs=pl.BlockSpec(memory_space=pltpu.VMEM),
        out_shape=jax.ShapeDtypeStruct((parts, channels, own), BF16),
        scratch_shapes=[pltpu.VMEM((parts, depth, own), BF16), pltpu.SemaphoreType.DMA((parts,))],
        compiler_params=pltpu.CompilerParams(vmem_limit_bytes=18 << 20),
        cost_estimate=pl.CostEstimate(flops=800_000_000, bytes_accessed=14_000_000, transcendentals=0),
        name="long_parts",
    )(p, pltpu.with_memory_space_constraint(table, pltpu.HBM))


def prepare_kernel(
    ka_ref, halo_ref, mix_ref, grad_ref, index_ref, weight_ref, count_ref,
    rows_ref, send_ref, masked_ref, *refs,
):
    *slots_refs, picked_ref, held_ref, wide_ref, sem = refs
    channels = mix_ref.shape[0]
    wide_ref[channels:, :] = jnp.zeros((LANES - channels, channels), BF16)
    wide_ref[:channels, :] = mix_ref[...]
    atoms = grad_ref.shape[1]
    block = math.gcd(atoms, 512)
    sends, per_side = send_ref.shape[0], halo_ref.shape[1]

    def mix(i, carry):
        first = pl.multiple_of(i * block, block)
        mixed = lax.dot_general(
            grad_ref[:, pl.ds(first, block)], wide_ref[...], (((0,), (1,)), ((), ())),
            preferred_element_type=F32,
        )
        held_ref[pl.ds(first, block), :] = mixed.astype(BF16).astype(F32)
        return carry

    lax.fori_loop(0, atoms // block, mix, 0)
    leave = pltpu.make_async_copy(held_ref, rows_ref.at[pl.ds(0, atoms)], sem)
    leave.start()

    for side in range(2):
        for j in range(per_side):
            picked_ref[side * per_side + j, :] = held_ref[halo_ref[side, j], :]
    send_ref[...] = picked_ref[...].astype(BF16)

    slot = lax.broadcasted_iota(jnp.int32, weight_ref.shape, 0)
    masked = jnp.where(slot < count_ref[...], weight_ref[...], 0.0)
    for piece, slots_ref in enumerate(slots_refs):
        cut = slice(piece * LANES, (piece + 1) * LANES)
        slots_ref[:, : index_ref.shape[0]] = index_ref[:, cut].T
        masked_ref[cut, :] = masked[:, cut].T
    leave.wait()


def prepare(ka, mix, grad, index, weight, count, halo):
    channels, atoms = grad.shape
    slots = index.shape[0]
    per_side = halo.shape[1]
    own = atoms // lax.axis_size("ka")
    whole = pl.BlockSpec(memory_space=pltpu.VMEM)
    return pl.pallas_call(
        prepare_kernel,
        grid_spec=pltpu.PrefetchScalarGridSpec(
            num_scalar_prefetch=1,
            grid=(1,),
            in_specs=[
                pl.BlockSpec(memory_space=pltpu.SMEM),
                whole,
                whole,
                pl.BlockSpec((slots, own), lambda i, ka: (0, ka[0])),
                pl.BlockSpec((slots, own), lambda i, ka: (0, ka[0])),
                pl.BlockSpec((1, own), lambda i, ka: (0, ka[0])),
            ],
            out_specs=[pl.BlockSpec(memory_space=pltpu.HBM)] + [whole] * (2 + own // LANES),
            scratch_shapes=[
                pltpu.VMEM((2 * per_side, LANES), F32),
                pltpu.VMEM((atoms, LANES), F32),
                pltpu.VMEM((LANES, channels), BF16),
                pltpu.SemaphoreType.DMA(()),
            ],
        ),
        out_shape=[
            pltpu.HBM((atoms + 2 * per_side, LANES), F32),
            jax.ShapeDtypeStruct((2 * per_side, LANES), BF16),
            jax.ShapeDtypeStruct((own, slots), F32),
        ]
        + [jax.ShapeDtypeStruct((LANES, LANES), jnp.int32)] * (own // LANES),
        compiler_params=pltpu.CompilerParams(vmem_limit_bytes=12 << 20),
        cost_estimate=pl.CostEstimate(flops=1_000_000_000, bytes_accessed=8_000_000, transcendentals=0),
        name="prepare",
    )(ka, halo, mix, grad, index, weight, count)


def short_kernel(index_ref, weight_ref, rows_ref, out_ref, sums_ref, sems, *windows):
    sublane = lax.broadcasted_iota(jnp.int32, (8, LANES), 0)
    groups, depth = LANES // 8, len(windows)

    def fetch(g, w):
        block = index_ref.at[pl.ds(pl.multiple_of(g * 8, 8), 8)]
        return pltpu.make_async_copy(block, windows[w], sems.at[w])

    for w in range(depth):
        fetch(w, w).start()

    def round_of_groups(i, carry):
        for w in range(depth):
            g = i * depth + w
            fetch(g, w).wait()
            first = pl.multiple_of(g * 8, 8)
            weights = weight_ref[pl.ds(first, 8), :]
            total = jnp.zeros((8, LANES), F32)
            for s in range(weight_ref.shape[1]):
                picked = jnp.broadcast_to(rows_ref[windows[w][0, s]], (8, LANES))
                for a in range(1, 8):
                    row = jnp.broadcast_to(rows_ref[windows[w][a, s]], (8, LANES))
                    picked = jnp.where(sublane == a, row, picked)
                total = total + picked * weights[:, s : s + 1]
            sums_ref[pl.ds(first, 8), :] = total

            @pl.when(g + depth < groups)
            def _(g=g, w=w):
                fetch(g + depth, w).start()

        return carry

    lax.fori_loop(0, groups // depth, round_of_groups, 0)
    out_ref[...] = sums_ref[...].T[: out_ref.shape[0], :]


def short_sums(piece, channels, index, weight, rows, flops, depth=4):
    slots = weight.shape[1]
    return pl.pallas_call(
        short_kernel,
        grid=(1,),
        in_specs=[
            pl.BlockSpec(memory_space=pltpu.VMEM),
            pl.BlockSpec((LANES, slots), lambda i: (piece, 0)),
            pl.BlockSpec(memory_space=pltpu.VMEM),
        ],
        out_specs=pl.BlockSpec(memory_space=pltpu.VMEM),
        out_shape=jax.ShapeDtypeStruct((channels, LANES), F32),
        scratch_shapes=[pltpu.VMEM((LANES, LANES), F32), pltpu.SemaphoreType.DMA((depth,))]
        + [pltpu.SMEM((8, LANES), jnp.int32)] * depth,
        compiler_params=pltpu.CompilerParams(vmem_limit_bytes=6 << 20),
        cost_estimate=pl.CostEstimate(flops=flops, bytes_accessed=400_000, transcendentals=0),
        name="short_sums",
    )(index, weight, rows)


def local(
    grad_out,
    frac_pos,
    k_index,
    ewald_filter,
    struct_fac,
    out_weight,
    pair_mix,
    pair_weight,
    nbr_index,
    nbr_count,
    halo_send,
):
    channels, local_atoms = grad_out.shape
    ka_size, dom_size = lax.axis_size("ka"), lax.axis_size("dom")
    own_rows = local_atoms // ka_size
    k_count = k_index.shape[1]

    ka = lax.axis_index("ka").astype(jnp.int32)
    rows, send, masked, *slots = prepare(
        ka[None],
        pair_mix,
        *(
            pltpu.with_memory_space_constraint(a, pltpu.HBM)
            for a in (grad_out, nbr_index, pair_weight, nbr_count[None, :], halo_send)
        ),
    )
    per_side = halo_send.shape[1]
    from_left = shifted(send[:per_side], "dom", 1)
    from_right = shifted(send[per_side:], "dom", -1)
    short = []

    def short_piece(flops):
        piece = len(short)
        short.append(short_sums(piece, channels, slots[piece], masked, extended, flops))

    def beside(value, flips, pieces):
        nonlocal slots
        value, slots = lax.optimization_barrier((value, slots))
        received = [swapped(value, "dom", flip) for flip in flips]
        start = len(short)
        for _ in range(pieces):
            short_piece(4_000_000_000)
        received, short[start:] = lax.optimization_barrier((received, short[start:]))
        return [r.astype(F32) for r in received]

    k_rows = k_index.astype(BF16).T
    k_triple = jnp.concatenate([k_rows, k_rows, k_rows, jnp.zeros((k_count, 7), BF16)], axis=1)
    frac_late, send_late = lax.optimization_barrier((frac_pos, send))
    q, table = front(out_weight, grad_out, frac_late, k_triple)
    q, from_left, from_right = lax.optimization_barrier((q, from_left, from_right))
    ghosts = jnp.concatenate([from_left, from_right], axis=0).astype(F32)
    extended = lax.dynamic_update_slice_in_dim(rows, ghosts, local_atoms, 0)
    extended = lax.optimization_barrier(extended)[:, None, :]

    half = channels // 2
    core = lax.axis_index("dom") % 2
    mine = lax.dynamic_slice_in_dim(q, core * half, half, 0)
    other = lax.dynamic_slice_in_dim(q, (1 - core) * half, half, 0)
    total = mine + beside(other.astype(BF16), [1], 0)[0]
    bit = 2
    while bit < dom_size:
        rounded = total.astype(BF16)
        total = rounded.astype(F32)
        if 2 * bit < dom_size:
            first, second, third = beside(rounded, [bit, 2 * bit, 3 * bit], 1 if bit == 2 else 2)
            total = (total + first) + (second + third)
        else:
            total = total + beside(rounded, [bit], 1)[0]
        bit *= 4
    partner = beside(total, [1], 0)[0]
    q = jnp.where(
        core == 0,
        jnp.concatenate([total, partner], axis=0),
        jnp.concatenate([partner, total], axis=0),
    )
    q_cos, q_sin = q[:, :k_count], q[:, k_count:]
    atom_total = local_atoms * dom_size
    d_filter = (struct_fac[0] * q_cos + struct_fac[1] * q_sin) / atom_total
    p = jnp.concatenate([ewald_filter * q_cos, ewald_filter * q_sin], axis=1).astype(BF16)

    parts = long_parts(p, table, ka_size)
    parts, slots = lax.optimization_barrier((parts, slots))
    parts = lax.all_to_all(parts, "ka", 0, 0, tiled=True)
    while len(short) < own_rows // LANES:
        short_piece(100_000_000)
    long_own = jnp.sum(parts.astype(F32), axis=0)
    own_grad = lax.dynamic_slice_in_dim(grad_out, ka * own_rows, own_rows, 1).astype(F32)
    d_feat = (own_grad + long_own + jnp.concatenate(short, axis=1)).astype(BF16)
    return (d_feat, d_filter)


def solution(mesh):
    return jax.shard_map(
        local,
        mesh=mesh,
        in_specs=(
            P(None, "dom"),
            P(None, "dom"),
            P(None, "ka"),
            P(None, "ka"),
            P(None, None, "ka"),
            P(),
            P(),
            P(None, "dom"),
            P(None, "dom"),
            P("dom"),
            P(None, "dom"),
        ),
        out_specs=(P(None, ("dom", "ka")), P(None, "ka")),
        check_vma=False,
    )
```

```python
import functools
import math

import jax
import jax.numpy as jnp
import numpy as np
from jax import lax
from jax.experimental import pallas as pl
from jax.experimental.pallas import tpu as pltpu
from jax.sharding import PartitionSpec as P

BF16 = jnp.bfloat16
F32 = jnp.float32
LANES = 128


def even_fit(function, terms):
    u = np.cos(np.pi * (np.arange(200) + 0.5) / 200) * 0.125 + 0.125
    fitted = np.polynomial.chebyshev.Chebyshev.fit(u, function(np.sqrt(u)), terms - 1, domain=[0, 0.25])
    return [float(c) for c in fitted.convert(kind=np.polynomial.Polynomial).coef]


SIN_HALF = even_fit(lambda r: math.sqrt(2) * np.sin(np.pi * r) / r, 3)
COS_HALF = even_fit(lambda r: math.sqrt(2) * np.cos(np.pi * r), 4)


def swapped(block, axis, bit):
    return lax.ppermute(block, axis, [(i, i ^ bit) for i in range(lax.axis_size(axis))])


def shifted(block, axis, distance):
    devices = range(lax.axis_size(axis))
    route = [((i - distance) % len(devices), i) for i in devices]
    return lax.ppermute(block, axis, route)


def front_kernel(
    rows, tile, mix_ref, grad_ref, frac_ref, k_ref,
    q_ref, whole_ref, pieces_ref, even_ref, odd_ref, held_ref, sems,
):
    step, last = pl.program_id(0), pl.num_programs(0) - 1
    slot = lax.rem(step, 2)
    table_ref = held_ref.at[slot]
    block = grad_ref.shape[1]
    k_count = k_ref.shape[0]
    turns_refs = (even_ref, odd_ref)

    def keep(at, slot):
        columns = pl.ds(pl.multiple_of(at * block, block), block)
        return pltpu.make_async_copy(held_ref.at[slot], whole_ref.at[:, columns], sems.at[slot])

    @pl.when(step == 0)
    def _():
        q_ref[...] = jnp.zeros_like(q_ref)
        pieces_ref[...] = jnp.zeros_like(pieces_ref)

    @pl.when(step >= 2)
    def _():
        keep(step - 2, slot).wait()

    frac = frac_ref[...]
    high = frac.astype(BF16).astype(F32)
    rest = frac - high
    middle = rest.astype(BF16).astype(F32)
    pieces_ref[0:3, :] = high
    pieces_ref[3:6, :] = middle
    pieces_ref[6:9, :] = rest - middle
    pieces = pieces_ref[...].astype(BF16)
    cot = jnp.dot(mix_ref[...], grad_ref[...], preferred_element_type=F32).astype(BF16)

    def turn(t):
        k_tile = k_ref[t * tile : (t + 1) * tile, :]
        turns_refs[t % 2][...] = jnp.dot(k_tile, pieces, preferred_element_type=F32)

    def fill(t):
        for row in range(0, tile, rows):
            turns = turns_refs[t % 2][row : row + rows, :]
            r = turns - jnp.round(turns)
            u = r * r
            s = SIN_HALF[-1]
            for coefficient in SIN_HALF[-2::-1]:
                s = s * u + coefficient
            s = s * r
            c = COS_HALF[-1]
            for coefficient in COS_HALF[-2::-1]:
                c = c * u + coefficient
            first = t * tile + row
            table_ref[first : first + rows, :] = (1.0 - s * s).astype(BF16)
            table_ref[k_count + first : k_count + first + rows, :] = (s * c).astype(BF16)

    def add(t):
        for first in (t * tile, k_count + t * tile):
            q_ref[:, first : first + tile] += lax.dot_general(
                cot, table_ref[first : first + tile, :], (((1,), (1,)), ((), ())),
                preferred_element_type=F32,
            )

    tiles = k_count // tile
    turn(0)
    for t in range(tiles):
        if t > 0:
            add(t - 1)
        if t + 1 < tiles:
            turn(t + 1)
        fill(t)
    add(tiles - 1)
    keep(step, slot).start()

    @pl.when(step == last)
    def _():
        keep(step - 1, 1 - slot).wait()
        keep(step, slot).wait()


def front(mix, grad, frac, k_triple, rows=16, tile=128, block=1024):
    channels, atoms = grad.shape
    k_count = k_triple.shape[0]
    return pl.pallas_call(
        functools.partial(front_kernel, rows, tile),
        grid=(atoms // block,),
        in_specs=[
            pl.BlockSpec((channels, channels), lambda i: (0, 0)),
            pl.BlockSpec((channels, block), lambda i: (0, i)),
            pl.BlockSpec((3, block), lambda i: (0, i)),
            pl.BlockSpec((k_count, 16), lambda i: (0, 0)),
        ],
        out_specs=[
            pl.BlockSpec((channels, 2 * k_count), lambda i: (0, 0)),
            pl.BlockSpec(memory_space=pltpu.HBM),
        ],
        out_shape=[
            jax.ShapeDtypeStruct((channels, 2 * k_count), F32),
            pltpu.HBM((2 * k_count, atoms), BF16),
        ],
        scratch_shapes=[
            pltpu.VMEM((16, block), F32),
            pltpu.VMEM((tile, block), F32),
            pltpu.VMEM((tile, block), F32),
            pltpu.VMEM((2, 2 * k_count, block), BF16),
            pltpu.SemaphoreType.DMA((2,)),
        ],
        compiler_params=pltpu.CompilerParams(vmem_limit_bytes=12 << 20),
        cost_estimate=pl.CostEstimate(flops=20_000_000_000, bytes_accessed=14_000_000, transcendentals=0),
        name="structure_sums",
    )(mix, grad, frac, k_triple)


def long_kernel(p_ref, table_ref, out_ref, held_ref, sems):
    parts, _, own = out_ref.shape
    fetches = [
        pltpu.make_async_copy(
            table_ref.at[:, at * own : (at + 1) * own], held_ref.at[at], sems.at[at]
        )
        for at in range(parts)
    ]
    for fetch in fetches:
        fetch.start()
    for at, fetch in enumerate(fetches):
        fetch.wait()
        out_ref[at] = jnp.dot(p_ref[...], held_ref[at], preferred_element_type=F32).astype(BF16)


def long_parts(p, table, parts):
    channels, depth = p.shape
    own = table.shape[1] // parts
    return pl.pallas_call(
        long_kernel,
        in_specs=[pl.BlockSpec(memory_space=pltpu.VMEM), pl.BlockSpec(memory_space=pltpu.HBM)],
        out_specs=pl.BlockSpec(memory_space=pltpu.VMEM),
        out_shape=jax.ShapeDtypeStruct((parts, channels, own), BF16),
        scratch_shapes=[pltpu.VMEM((parts, depth, own), BF16), pltpu.SemaphoreType.DMA((parts,))],
        compiler_params=pltpu.CompilerParams(vmem_limit_bytes=18 << 20),
        cost_estimate=pl.CostEstimate(flops=800_000_000, bytes_accessed=14_000_000, transcendentals=0),
        name="long_parts",
    )(p, pltpu.with_memory_space_constraint(table, pltpu.HBM))


def prepare_kernel(
    ka_ref, halo_ref, mix_ref, grad_ref, index_ref, weight_ref, count_ref,
    rows_ref, send_ref, masked_ref, *refs,
):
    *slots_refs, picked_ref, held_ref, wide_ref, sem = refs
    channels = mix_ref.shape[0]
    wide_ref[channels:, :] = jnp.zeros((LANES - channels, channels), BF16)
    wide_ref[:channels, :] = mix_ref[...]
    atoms = grad_ref.shape[1]
    block = math.gcd(atoms, 512)
    sends, per_side = send_ref.shape[0], halo_ref.shape[1]

    def mix(i, carry):
        first = pl.multiple_of(i * block, block)
        mixed = lax.dot_general(
            grad_ref[:, pl.ds(first, block)], wide_ref[...], (((0,), (1,)), ((), ())),
            preferred_element_type=F32,
        )
        held_ref[pl.ds(first, block), :] = mixed.astype(BF16).astype(F32)
        return carry

    lax.fori_loop(0, atoms // block, mix, 0)
    leave = pltpu.make_async_copy(held_ref, rows_ref.at[pl.ds(0, atoms)], sem)
    leave.start()

    for side in range(2):
        for j in range(per_side):
            picked_ref[side * per_side + j, :] = held_ref[halo_ref[side, j], :]
    send_ref[...] = picked_ref[...].astype(BF16)

    slot = lax.broadcasted_iota(jnp.int32, weight_ref.shape, 0)
    masked = jnp.where(slot < count_ref[...], weight_ref[...], 0.0)
    for piece, slots_ref in enumerate(slots_refs):
        cut = slice(piece * LANES, (piece + 1) * LANES)
        slots_ref[:, : index_ref.shape[0]] = index_ref[:, cut].T
        masked_ref[cut, :] = masked[:, cut].T
    leave.wait()


def prepare(ka, mix, grad, index, weight, count, halo):
    channels, atoms = grad.shape
    slots = index.shape[0]
    per_side = halo.shape[1]
    own = atoms // lax.axis_size("ka")
    whole = pl.BlockSpec(memory_space=pltpu.VMEM)
    return pl.pallas_call(
        prepare_kernel,
        grid_spec=pltpu.PrefetchScalarGridSpec(
            num_scalar_prefetch=1,
            grid=(1,),
            in_specs=[
                pl.BlockSpec(memory_space=pltpu.SMEM),
                whole,
                whole,
                pl.BlockSpec((slots, own), lambda i, ka: (0, ka[0])),
                pl.BlockSpec((slots, own), lambda i, ka: (0, ka[0])),
                pl.BlockSpec((1, own), lambda i, ka: (0, ka[0])),
            ],
            out_specs=[pl.BlockSpec(memory_space=pltpu.HBM)] + [whole] * (2 + own // LANES),
            scratch_shapes=[
                pltpu.VMEM((2 * per_side, LANES), F32),
                pltpu.VMEM((atoms, LANES), F32),
                pltpu.VMEM((LANES, channels), BF16),
                pltpu.SemaphoreType.DMA(()),
            ],
        ),
        out_shape=[
            pltpu.HBM((atoms + 2 * per_side, LANES), F32),
            jax.ShapeDtypeStruct((2 * per_side, LANES), BF16),
            jax.ShapeDtypeStruct((own, slots), F32),
        ]
        + [jax.ShapeDtypeStruct((LANES, LANES), jnp.int32)] * (own // LANES),
        compiler_params=pltpu.CompilerParams(vmem_limit_bytes=12 << 20),
        cost_estimate=pl.CostEstimate(flops=1_000_000_000, bytes_accessed=8_000_000, transcendentals=0),
        name="prepare",
    )(ka, halo, mix, grad, index, weight, count)


def short_kernel(start, index_ref, weight_ref, rows_ref, out_ref, sums_ref, sems, *windows):
    sublane = lax.broadcasted_iota(jnp.int32, (8, LANES), 0)
    groups, depth = LANES // 8, len(windows)

    def fetch(g, w):
        block = index_ref.at[pl.ds(pl.multiple_of(g * 8, 8), 8)]
        return pltpu.make_async_copy(block, windows[w], sems.at[w])

    for w in range(depth):
        fetch(w, w).start()

    def round_of_groups(i, carry):
        for w in range(depth):
            g = i * depth + w
            fetch(g, w).wait()
            first = pl.multiple_of(g * 8, 8)
            weights = weight_ref[pl.ds(start + first, 8), :]
            total = jnp.zeros((8, LANES), F32)
            for s in range(weight_ref.shape[1]):
                picked = jnp.broadcast_to(rows_ref[windows[w][0, s]], (8, LANES))
                for a in range(1, 8):
                    row = jnp.broadcast_to(rows_ref[windows[w][a, s]], (8, LANES))
                    picked = jnp.where(sublane == a, row, picked)
                total = total + picked * weights[:, s : s + 1]
            sums_ref[pl.ds(first, 8), :] = total

            @pl.when(g + depth < groups)
            def _(g=g, w=w):
                fetch(g + depth, w).start()

        return carry

    lax.fori_loop(0, groups // depth, round_of_groups, 0)
    out_ref[...] = sums_ref[...].T[: out_ref.shape[0], :]


def short_sums(piece, channels, index, weight, rows, flops, depth=4):
    return pl.pallas_call(
        functools.partial(short_kernel, piece * LANES),
        in_specs=[pl.BlockSpec(memory_space=pltpu.VMEM)] * 3,
        out_specs=pl.BlockSpec(memory_space=pltpu.VMEM),
        out_shape=jax.ShapeDtypeStruct((channels, LANES), F32),
        scratch_shapes=[pltpu.VMEM((LANES, LANES), F32), pltpu.SemaphoreType.DMA((depth,))]
        + [pltpu.SMEM((8, LANES), jnp.int32)] * depth,
        compiler_params=pltpu.CompilerParams(vmem_limit_bytes=6 << 20),
        cost_estimate=pl.CostEstimate(flops=flops, bytes_accessed=400_000, transcendentals=0),
        name="short_sums",
    )(index, weight, rows)


def near_kernel(index_ref, rows_ref, out_ref):
    out_ref[...] = index_ref[...]


def near(index, rows):
    return pl.pallas_call(
        near_kernel,
        in_specs=[pl.BlockSpec(memory_space=pltpu.VMEM)] * 2,
        out_specs=pl.BlockSpec(memory_space=pltpu.VMEM),
        out_shape=jax.ShapeDtypeStruct(index.shape, index.dtype),
        compiler_params=pltpu.CompilerParams(vmem_limit_bytes=6 << 20),
        cost_estimate=pl.CostEstimate(flops=1_000_000_000, bytes_accessed=400_000, transcendentals=0),
        name="near",
    )(index, rows)


def local(
    grad_out,
    frac_pos,
    k_index,
    ewald_filter,
    struct_fac,
    out_weight,
    pair_mix,
    pair_weight,
    nbr_index,
    nbr_count,
    halo_send,
):
    channels, local_atoms = grad_out.shape
    ka_size, dom_size = lax.axis_size("ka"), lax.axis_size("dom")
    own_rows = local_atoms // ka_size
    k_count = k_index.shape[1]

    ka = lax.axis_index("ka").astype(jnp.int32)
    rows, send, masked, *slots = prepare(
        ka[None],
        pair_mix,
        *(
            pltpu.with_memory_space_constraint(a, pltpu.HBM)
            for a in (grad_out, nbr_index, pair_weight, nbr_count[None, :], halo_send)
        ),
    )
    per_side = halo_send.shape[1]
    from_left = shifted(send[:per_side], "dom", 1)
    from_right = shifted(send[per_side:], "dom", -1)
    short = []

    def short_piece(flops):
        piece = len(short)
        short.append(short_sums(piece, channels, slots[piece], masked, extended, flops))

    def beside(value, bit, pieces):
        nonlocal slots
        value, slots = lax.optimization_barrier((value, slots))
        received = swapped(value, "dom", bit)
        start = len(short)
        if not pieces and bit == 2:
            slots[0] = near(slots[0], extended)
            received, slots[0] = lax.optimization_barrier((received, slots[0]))
        for _ in range(pieces):
            short_piece(4_000_000_000)
        received, short[start:] = lax.optimization_barrier((received, short[start:]))
        return received.astype(F32)

    k_rows = k_index.astype(BF16).T
    k_triple = jnp.concatenate([k_rows, k_rows, k_rows, jnp.zeros((k_count, 7), BF16)], axis=1)
    frac_late, send_late = lax.optimization_barrier((frac_pos, send))
    q, table = front(out_weight, grad_out, frac_late, k_triple)
    q, from_left, from_right = lax.optimization_barrier((q, from_left, from_right))
    ghosts = jnp.concatenate([from_left, from_right], axis=0).astype(F32)
    extended = lax.dynamic_update_slice_in_dim(rows, ghosts, local_atoms, 0)
    extended = lax.optimization_barrier(extended)[:, None, :]

    half = channels // 2
    core = lax.axis_index("dom") % 2
    mine = lax.dynamic_slice_in_dim(q, core * half, half, 0)
    other = lax.dynamic_slice_in_dim(q, (1 - core) * half, half, 0)
    total = mine + beside(other.astype(BF16), 1, 0)
    bit = 2
    while bit < dom_size:
        rounded = total.astype(BF16)
        total = rounded.astype(F32) + beside(rounded, bit, 0 if bit == 2 else 1)
        bit *= 2
    partner = beside(total, 1, 0)
    q = jnp.where(
        core == 0,
        jnp.concatenate([total, partner], axis=0),
        jnp.concatenate([partner, total], axis=0),
    )
    q_cos, q_sin = q[:, :k_count], q[:, k_count:]
    atom_total = local_atoms * dom_size
    d_filter = (struct_fac[0] * q_cos + struct_fac[1] * q_sin) / atom_total
    p = jnp.concatenate([ewald_filter * q_cos, ewald_filter * q_sin], axis=1).astype(BF16)

    parts = long_parts(p, table, ka_size)
    parts, slots = lax.optimization_barrier((parts, slots))
    parts = lax.all_to_all(parts, "ka", 0, 0, tiled=True)
    while len(short) < own_rows // LANES:
        short_piece(100_000_000)
    long_own = jnp.sum(parts.astype(F32), axis=0)
    own_grad = lax.dynamic_slice_in_dim(grad_out, ka * own_rows, own_rows, 1).astype(F32)
    d_feat = (own_grad + long_own + jnp.concatenate(short, axis=1)).astype(BF16)
    return (d_feat, d_filter)


def solution(mesh):
    return jax.shard_map(
        local,
        mesh=mesh,
        in_specs=(
            P(None, "dom"),
            P(None, "dom"),
            P(None, "ka"),
            P(None, "ka"),
            P(None, None, "ka"),
            P(),
            P(),
            P(None, "dom"),
            P(None, "dom"),
            P("dom"),
            P(None, "dom"),
        ),
        out_specs=(P(None, ("dom", "ka")), P(None, "ka")),
        check_vma=False,
    )
```

```python
import functools
import math

import jax
import jax.numpy as jnp
import numpy as np
from jax import lax
from jax.experimental import pallas as pl
from jax.experimental.pallas import tpu as pltpu
from jax.sharding import PartitionSpec as P

BF16 = jnp.bfloat16
F32 = jnp.float32
LANES = 128


def even_fit(function, terms):
    u = np.cos(np.pi * (np.arange(200) + 0.5) / 200) * 0.125 + 0.125
    fitted = np.polynomial.chebyshev.Chebyshev.fit(u, function(np.sqrt(u)), terms - 1, domain=[0, 0.25])
    return [float(c) for c in fitted.convert(kind=np.polynomial.Polynomial).coef]


SIN_HALF = even_fit(lambda r: math.sqrt(2) * np.sin(np.pi * r) / r, 3)
COS_HALF = even_fit(lambda r: math.sqrt(2) * np.cos(np.pi * r), 4)


def swapped(block, axis, bit):
    return lax.ppermute(block, axis, [(i, i ^ bit) for i in range(lax.axis_size(axis))])


def shifted(block, axis, distance):
    devices = range(lax.axis_size(axis))
    route = [((i - distance) % len(devices), i) for i in devices]
    return lax.ppermute(block, axis, route)


def front_kernel(
    rows, tile, mix_ref, grad_ref, frac_ref, k_ref,
    q_ref, whole_ref, pieces_ref, even_ref, odd_ref, held_ref, sems,
):
    step, last = pl.program_id(0), pl.num_programs(0) - 1
    slot = lax.rem(step, 2)
    table_ref = held_ref.at[slot]
    block = grad_ref.shape[1]
    k_count = k_ref.shape[0]
    turns_refs = (even_ref, odd_ref)

    def keep(at, slot):
        columns = pl.ds(pl.multiple_of(at * block, block), block)
        return pltpu.make_async_copy(held_ref.at[slot], whole_ref.at[:, columns], sems.at[slot])

    @pl.when(step == 0)
    def _():
        q_ref[...] = jnp.zeros_like(q_ref)
        pieces_ref[...] = jnp.zeros_like(pieces_ref)

    @pl.when(step >= 2)
    def _():
        keep(step - 2, slot).wait()

    frac = frac_ref[...]
    high = frac.astype(BF16).astype(F32)
    rest = frac - high
    middle = rest.astype(BF16).astype(F32)
    pieces_ref[0:3, :] = high
    pieces_ref[3:6, :] = middle
    pieces_ref[6:9, :] = rest - middle
    pieces = pieces_ref[...].astype(BF16)
    cot = jnp.dot(mix_ref[...], grad_ref[...], preferred_element_type=F32).astype(BF16)

    def turn(t):
        k_tile = k_ref[t * tile : (t + 1) * tile, :]
        turns_refs[t % 2][...] = jnp.dot(k_tile, pieces, preferred_element_type=F32)

    def fill(t):
        for row in range(0, tile, rows):
            turns = turns_refs[t % 2][row : row + rows, :]
            r = turns - jnp.round(turns)
            u = r * r
            s = SIN_HALF[-1]
            for coefficient in SIN_HALF[-2::-1]:
                s = s * u + coefficient
            s = s * r
            c = COS_HALF[-1]
            for coefficient in COS_HALF[-2::-1]:
                c = c * u + coefficient
            first = t * tile + row
            table_ref[first : first + rows, :] = (1.0 - s * s).astype(BF16)
            table_ref[k_count + first : k_count + first + rows, :] = (s * c).astype(BF16)

    def add(t):
        for first in (t * tile, k_count + t * tile):
            q_ref[:, first : first + tile] += lax.dot_general(
                cot, table_ref[first : first + tile, :], (((1,), (1,)), ((), ())),
                preferred_element_type=F32,
            )

    tiles = k_count // tile
    turn(0)
    for t in range(tiles):
        if t > 0:
            add(t - 1)
        if t + 1 < tiles:
            turn(t + 1)
        fill(t)
    add(tiles - 1)
    keep(step, slot).start()

    @pl.when(step == last)
    def _():
        keep(step - 1, 1 - slot).wait()
        keep(step, slot).wait()


def front(mix, grad, frac, k_triple, rows=16, tile=128, block=1024):
    channels, atoms = grad.shape
    k_count = k_triple.shape[0]
    return pl.pallas_call(
        functools.partial(front_kernel, rows, tile),
        grid=(atoms // block,),
        in_specs=[
            pl.BlockSpec((channels, channels), lambda i: (0, 0)),
            pl.BlockSpec((channels, block), lambda i: (0, i)),
            pl.BlockSpec((3, block), lambda i: (0, i)),
            pl.BlockSpec((k_count, 16), lambda i: (0, 0)),
        ],
        out_specs=[
            pl.BlockSpec((channels, 2 * k_count), lambda i: (0, 0)),
            pl.BlockSpec(memory_space=pltpu.HBM),
        ],
        out_shape=[
            jax.ShapeDtypeStruct((channels, 2 * k_count), F32),
            pltpu.HBM((2 * k_count, atoms), BF16),
        ],
        scratch_shapes=[
            pltpu.VMEM((16, block), F32),
            pltpu.VMEM((tile, block), F32),
            pltpu.VMEM((tile, block), F32),
            pltpu.VMEM((2, 2 * k_count, block), BF16),
            pltpu.SemaphoreType.DMA((2,)),
        ],
        compiler_params=pltpu.CompilerParams(vmem_limit_bytes=12 << 20),
        cost_estimate=pl.CostEstimate(flops=20_000_000_000, bytes_accessed=14_000_000, transcendentals=0),
        name="structure_sums",
    )(mix, grad, frac, k_triple)


def long_kernel(p_ref, table_ref, out_ref, held_ref, sems):
    parts, _, own = out_ref.shape
    fetches = [
        pltpu.make_async_copy(
            table_ref.at[:, at * own : (at + 1) * own], held_ref.at[at], sems.at[at]
        )
        for at in range(parts)
    ]
    for fetch in fetches:
        fetch.start()
    for at, fetch in enumerate(fetches):
        fetch.wait()
        out_ref[at] = jnp.dot(p_ref[...], held_ref[at], preferred_element_type=F32).astype(BF16)


def long_parts(p, table, parts):
    channels, depth = p.shape
    own = table.shape[1] // parts
    return pl.pallas_call(
        long_kernel,
        in_specs=[pl.BlockSpec(memory_space=pltpu.VMEM), pl.BlockSpec(memory_space=pltpu.HBM)],
        out_specs=pl.BlockSpec(memory_space=pltpu.VMEM),
        out_shape=jax.ShapeDtypeStruct((parts, channels, own), BF16),
        scratch_shapes=[pltpu.VMEM((parts, depth, own), BF16), pltpu.SemaphoreType.DMA((parts,))],
        compiler_params=pltpu.CompilerParams(vmem_limit_bytes=18 << 20),
        cost_estimate=pl.CostEstimate(flops=800_000_000, bytes_accessed=14_000_000, transcendentals=0),
        name="long_parts",
    )(p, pltpu.with_memory_space_constraint(table, pltpu.HBM))


def prepare_kernel(
    ka_ref, halo_ref, mix_ref, grad_ref, index_ref, weight_ref, count_ref,
    rows_ref, send_ref, masked_ref, *refs,
):
    *slots_refs, picked_ref, held_ref, wide_ref, sem = refs
    channels = mix_ref.shape[0]
    wide_ref[channels:, :] = jnp.zeros((LANES - channels, channels), BF16)
    wide_ref[:channels, :] = mix_ref[...]
    atoms = grad_ref.shape[1]
    block = math.gcd(atoms, 512)
    sends, per_side = send_ref.shape[0], halo_ref.shape[1]

    def mix(i, carry):
        first = pl.multiple_of(i * block, block)
        mixed = lax.dot_general(
            grad_ref[:, pl.ds(first, block)], wide_ref[...], (((0,), (1,)), ((), ())),
            preferred_element_type=F32,
        )
        held_ref[pl.ds(first, block), :] = mixed.astype(BF16).astype(F32)
        return carry

    lax.fori_loop(0, atoms // block, mix, 0)
    leave = pltpu.make_async_copy(held_ref, rows_ref.at[pl.ds(0, atoms)], sem)
    leave.start()

    for side in range(2):
        for j in range(per_side):
            picked_ref[side * per_side + j, :] = held_ref[halo_ref[side, j], :]
    send_ref[...] = picked_ref[...].astype(BF16)

    slot = lax.broadcasted_iota(jnp.int32, weight_ref.shape, 0)
    masked = jnp.where(slot < count_ref[...], weight_ref[...], 0.0)
    for piece, slots_ref in enumerate(slots_refs):
        cut = slice(piece * LANES, (piece + 1) * LANES)
        slots_ref[:, : index_ref.shape[0]] = index_ref[:, cut].T
        masked_ref[cut, :] = masked[:, cut].T
    leave.wait()


def prepare(ka, mix, grad, index, weight, count, halo):
    channels, atoms = grad.shape
    slots = index.shape[0]
    per_side = halo.shape[1]
    own = atoms // lax.axis_size("ka")
    whole = pl.BlockSpec(memory_space=pltpu.VMEM)
    return pl.pallas_call(
        prepare_kernel,
        grid_spec=pltpu.PrefetchScalarGridSpec(
            num_scalar_prefetch=1,
            grid=(1,),
            in_specs=[
                pl.BlockSpec(memory_space=pltpu.SMEM),
                whole,
                whole,
                pl.BlockSpec((slots, own), lambda i, ka: (0, ka[0])),
                pl.BlockSpec((slots, own), lambda i, ka: (0, ka[0])),
                pl.BlockSpec((1, own), lambda i, ka: (0, ka[0])),
            ],
            out_specs=[pl.BlockSpec(memory_space=pltpu.HBM)] + [whole] * (2 + own // LANES),
            scratch_shapes=[
                pltpu.VMEM((2 * per_side, LANES), F32),
                pltpu.VMEM((atoms, LANES), F32),
                pltpu.VMEM((LANES, channels), BF16),
                pltpu.SemaphoreType.DMA(()),
            ],
        ),
        out_shape=[
            pltpu.HBM((atoms + 2 * per_side, LANES), F32),
            jax.ShapeDtypeStruct((2 * per_side, LANES), BF16),
            jax.ShapeDtypeStruct((own, slots), F32),
        ]
        + [jax.ShapeDtypeStruct((LANES, LANES), jnp.int32)] * (own // LANES),
        compiler_params=pltpu.CompilerParams(vmem_limit_bytes=12 << 20),
        cost_estimate=pl.CostEstimate(flops=1_000_000_000, bytes_accessed=8_000_000, transcendentals=0),
        name="prepare",
    )(ka, halo, mix, grad, index, weight, count)


def short_kernel(start, index_ref, weight_ref, rows_ref, out_ref, sums_ref, sems, *windows):
    sublane = lax.broadcasted_iota(jnp.int32, (8, LANES), 0)
    groups, depth = LANES // 8, len(windows)

    def fetch(g, w):
        block = index_ref.at[pl.ds(pl.multiple_of(g * 8, 8), 8)]
        return pltpu.make_async_copy(block, windows[w], sems.at[w])

    for w in range(depth):
        fetch(w, w).start()

    def round_of_groups(i, carry):
        for w in range(depth):
            g = i * depth + w
            fetch(g, w).wait()
            first = pl.multiple_of(g * 8, 8)
            weights = weight_ref[pl.ds(start + first, 8), :]
            total = jnp.zeros((8, LANES), F32)
            for s in range(weight_ref.shape[1]):
                picked = jnp.broadcast_to(rows_ref[windows[w][0, s]], (8, LANES))
                for a in range(1, 8):
                    row = jnp.broadcast_to(rows_ref[windows[w][a, s]], (8, LANES))
                    picked = jnp.where(sublane == a, row, picked)
                total = total + picked * weights[:, s : s + 1]
            sums_ref[pl.ds(first, 8), :] = total

            @pl.when(g + depth < groups)
            def _(g=g, w=w):
                fetch(g + depth, w).start()

        return carry

    lax.fori_loop(0, groups // depth, round_of_groups, 0)
    out_ref[...] = sums_ref[...].T[: out_ref.shape[0], :]


def short_sums(piece, channels, index, weight, rows, flops, depth=8):
    return pl.pallas_call(
        functools.partial(short_kernel, piece * LANES),
        in_specs=[pl.BlockSpec(memory_space=pltpu.VMEM)] * 3,
        out_specs=pl.BlockSpec(memory_space=pltpu.VMEM),
        out_shape=jax.ShapeDtypeStruct((channels, LANES), F32),
        scratch_shapes=[pltpu.VMEM((LANES, LANES), F32), pltpu.SemaphoreType.DMA((depth,))]
        + [pltpu.SMEM((8, LANES), jnp.int32)] * depth,
        compiler_params=pltpu.CompilerParams(vmem_limit_bytes=6 << 20),
        cost_estimate=pl.CostEstimate(flops=flops, bytes_accessed=400_000, transcendentals=0),
        name="short_sums",
    )(index, weight, rows)


def near_kernel(index_ref, rows_ref, out_ref):
    out_ref[...] = index_ref[...]


def near(index, rows):
    return pl.pallas_call(
        near_kernel,
        in_specs=[pl.BlockSpec(memory_space=pltpu.VMEM)] * 2,
        out_specs=pl.BlockSpec(memory_space=pltpu.VMEM),
        out_shape=jax.ShapeDtypeStruct(index.shape, index.dtype),
        compiler_params=pltpu.CompilerParams(vmem_limit_bytes=6 << 20),
        cost_estimate=pl.CostEstimate(flops=1_000_000_000, bytes_accessed=400_000, transcendentals=0),
        name="near",
    )(index, rows)


def local(
    grad_out,
    frac_pos,
    k_index,
    ewald_filter,
    struct_fac,
    out_weight,
    pair_mix,
    pair_weight,
    nbr_index,
    nbr_count,
    halo_send,
):
    channels, local_atoms = grad_out.shape
    ka_size, dom_size = lax.axis_size("ka"), lax.axis_size("dom")
    own_rows = local_atoms // ka_size
    k_count = k_index.shape[1]

    ka = lax.axis_index("ka").astype(jnp.int32)
    rows, send, masked, *slots = prepare(
        ka[None],
        pair_mix,
        *(
            pltpu.with_memory_space_constraint(a, pltpu.HBM)
            for a in (grad_out, nbr_index, pair_weight, nbr_count[None, :], halo_send)
        ),
    )
    per_side = halo_send.shape[1]
    from_left = shifted(send[:per_side], "dom", 1)
    from_right = shifted(send[per_side:], "dom", -1)
    short = []

    def short_piece(flops):
        piece = len(short)
        short.append(short_sums(piece, channels, slots[piece], masked, extended, flops))

    def beside(value, bit, pieces):
        nonlocal slots
        value, slots = lax.optimization_barrier((value, slots))
        received = swapped(value, "dom", bit)
        start = len(short)
        if not pieces and bit == 2:
            slots[0] = near(slots[0], extended)
            received, slots[0] = lax.optimization_barrier((received, slots[0]))
        for _ in range(pieces):
            short_piece(4_000_000_000)
        received, short[start:] = lax.optimization_barrier((received, short[start:]))
        return received.astype(F32)

    k_rows = k_index.astype(BF16).T
    k_triple = jnp.concatenate([k_rows, k_rows, k_rows, jnp.zeros((k_count, 7), BF16)], axis=1)
    frac_late, send_late = lax.optimization_barrier((frac_pos, send))
    q, table = front(out_weight, grad_out, frac_late, k_triple)
    q, from_left, from_right = lax.optimization_barrier((q, from_left, from_right))
    ghosts = jnp.concatenate([from_left, from_right], axis=0).astype(F32)
    extended = lax.dynamic_update_slice_in_dim(rows, ghosts, local_atoms, 0)
    extended = lax.optimization_barrier(extended)[:, None, :]

    half = channels // 2
    core = lax.axis_index("dom") % 2
    mine = lax.dynamic_slice_in_dim(q, core * half, half, 0)
    other = lax.dynamic_slice_in_dim(q, (1 - core) * half, half, 0)
    total = mine + beside(other.astype(BF16), 1, 0)
    bit = 2
    while bit < dom_size:
        rounded = total.astype(BF16)
        total = rounded.astype(F32) + beside(rounded, bit, 0 if bit == 2 else 1)
        bit *= 2
    partner = beside(total, 1, 0)
    q = jnp.where(
        core == 0,
        jnp.concatenate([total, partner], axis=0),
        jnp.concatenate([partner, total], axis=0),
    )
    q_cos, q_sin = q[:, :k_count], q[:, k_count:]
    atom_total = local_atoms * dom_size
    d_filter = (struct_fac[0] * q_cos + struct_fac[1] * q_sin) / atom_total
    p = jnp.concatenate([ewald_filter * q_cos, ewald_filter * q_sin], axis=1).astype(BF16)

    parts = long_parts(p, table, ka_size)
    parts, slots = lax.optimization_barrier((parts, slots))
    parts = lax.all_to_all(parts, "ka", 0, 0, tiled=True)
    while len(short) < own_rows // LANES:
        short_piece(100_000_000)
    long_own = jnp.sum(parts.astype(F32), axis=0)
    own_grad = lax.dynamic_slice_in_dim(grad_out, ka * own_rows, own_rows, 1).astype(F32)
    d_feat = (own_grad + long_own + jnp.concatenate(short, axis=1)).astype(BF16)
    return (d_feat, d_filter)


def solution(mesh):
    return jax.shard_map(
        local,
        mesh=mesh,
        in_specs=(
            P(None, "dom"),
            P(None, "dom"),
            P(None, "ka"),
            P(None, "ka"),
            P(None, None, "ka"),
            P(),
            P(),
            P(None, "dom"),
            P(None, "dom"),
            P("dom"),
            P(None, "dom"),
        ),
        out_specs=(P(None, ("dom", "ka")), P(None, "ka")),
        check_vma=False,
    )
```
